32 devices in a mesh: groups: 2 (over x), gx: 16 (over z, y, core).
Axes of the slice: x: 2, y: 2, z: 4, core: 2. Of those that a mesh axis runs over, the one named last changes fastest.
Arguments:
- velocity: float32 [3, 32, 4, 32, 128], P(None, ('groups', 'gx')), parts along dimension 1, may hold values from -6 to 6
- stress: float32 [6, 32, 4, 32, 128], P(None, ('groups', 'gx')), parts along dimension 1, may hold values from -6 to 6
- memory: float32 [6, 32, 4, 32, 128], P(None, ('groups', 'gx')), parts along dimension 1, may hold values from -4 to 4
- lame_lambda: float32 [32, 4, 32, 128], P(('groups', 'gx')), parts along dimension 0, may hold values from 1.5 to 2.5
- lame_mu: float32 [32, 4, 32, 128], P(('groups', 'gx')), parts along dimension 0, may hold values from 0.1 to 0.5
- buoyancy: float32 [32, 4, 32, 128], P(('groups', 'gx')), parts along dimension 0, may hold values from 0.7 to 1
- decay: float32 [32, 4, 32, 128], P(('groups', 'gx')), parts along dimension 0, may hold values from 0.3 to 0.95
- loss: float32 [32, 4, 32, 128], P(('groups', 'gx')), parts along dimension 0, may hold values from 0.1 to 1
- tile_lambda: bfloat16 [256, 256], P(('groups', 'gx')), parts along dimension 0, may hold values from 3 to 4.5
- tile_mu: bfloat16 [256, 256], P(('groups', 'gx')), parts along dimension 0, may hold values from 1 to 2
- tile_buoy: bfloat16 [256, 256], P(('groups', 'gx')), parts along dimension 0, may hold values from 0.3984375 to 0.59765625
- tile_dest: int32 [256], P(('groups', 'gx')), parts along dimension 0, may hold values from -1 to 15, as said below
- brick_tiles: int32 [32, 64], P(('groups', 'gx')), parts along dimension 0, may hold values from -1 to 127, as said below
- src_index: int32 [512], P(('groups', 'gx')), parts along dimension 0, may hold values from 0 to 16383
- src_wave: float32 [512, 2], P(('groups', 'gx')), parts along dimension 0, may hold values from -6 to 6
Outputs:
- new_velocity: float32 [3, 32, 4, 32, 128], P(None, ('groups', 'gx')), parts along dimension 1
- new_stress: float32 [6, 32, 4, 32, 128], P(None, ('groups', 'gx')), parts along dimension 1
- new_memory: float32 [6, 32, 4, 32, 128], P(None, ('groups', 'gx')), parts along dimension 1
The draws below stay inside these ranges and needn't reach their ends.
There are 2 independent parts, one for each index of `groups`. The reference program is written for one: setup_inputs(seed, part) draws one part's arguments, and reference() takes and returns one part's arrays. A program takes and returns all parts, laid end to end along the dimension named above; each array names one. Nothing has to cross between parts.
Inputs may be any that keep to these rules, and one draw needn't show every extreme that they name: `tile_dest`: the 8 tiles stored on one device name distinct bricks; a brick receives at most 8 tiles, and some brick exactly 8 in every draw. `brick_tiles`: row b holds, at distinct positions, exactly the tiles whose tile_dest is b, each once.
All inputs are finite; a program needn't handle non-finite values.
Results may differ from the reference program's by a relative error of at most 0.00075.
Values may be sent and summed in bfloat16 or wider, within the bound.
A program may use at most 64 MiB of HBM per device.

```python
import jax
import jax.numpy as jnp
from jax import lax

BX = 4
BY = 32
NZ = 128
PY = 8
TY = 8
TZ = 8
STEPS = 2
ELEMS_DEV = 16
PX = 2
BRICKS = 16
TILES_DEV = 8
TILES = 128
SUBS_Y = 4
SUBS_Z = 16
SUBS = 64
TCELLS = 256
NX = 8
NY = 256
ELEMS = 256


def route_tables(key):
    offset_key, place_key, heavy_key, chosen_key, load_key = jax.random.split(key, 5)
    middle = BRICKS // 2
    drawn = jax.random.permutation(offset_key, BRICKS - 4) + 2
    drawn = jnp.where(drawn >= middle, drawn + 1, drawn)
    others = drawn[:TILES_DEV - 3].astype(jnp.int32)
    offsets = jnp.concatenate([jnp.array([1, BRICKS - 1, middle], jnp.int32), others]).astype(jnp.int32)
    places = jax.random.permutation(place_key, SUBS)[:TILES_DEV].astype(jnp.int32)
    heavy = jax.random.randint(heavy_key, (BRICKS,), 0, 2) == 0
    chosen = jax.random.randint(chosen_key, (), 0, BRICKS)
    heavy = heavy | (jnp.arange(BRICKS) == chosen)
    lighter = jax.random.randint(load_key, (BRICKS,), TILES_DEV // 2, TILES_DEV + 1)
    loads = jnp.where(heavy, TILES_DEV, lighter).astype(jnp.int32)
    return (offsets, places, loads)


def draw_tile_dest(key, part):
    offsets, places, loads = route_tables(jax.random.fold_in(key, 11))
    source = jnp.arange(BRICKS, dtype=jnp.int32)[:, None]
    target = (source + offsets[None, :]) % BRICKS
    slot_ids = jnp.arange(TILES_DEV, dtype=jnp.int32)[None, :]
    live = slot_ids < loads[target]
    return jnp.where(live, target, -1).reshape(-1).astype(jnp.int32)


def draw_brick_tiles(key, part):
    offsets, places, loads = route_tables(jax.random.fold_in(key, 11))
    bricks = jnp.arange(BRICKS, dtype=jnp.int32)[:, None]
    slot_ids = jnp.arange(TILES_DEV, dtype=jnp.int32)[None, :]
    source = (bricks - offsets[None, :]) % BRICKS
    idents = source * TILES_DEV + slot_ids
    values = jnp.where(slot_ids < loads[:, None], idents, -1).astype(jnp.int32)
    table = jnp.full((BRICKS, SUBS), -1, jnp.int32)
    return table.at[:, places].set(values)


def place_ends(entries, stream_key, low, largest):
    longest = entries.shape.index(max(entries.shape))
    spots = []
    for shift in (0, 1):
        where = [jax.random.randint(jax.random.fold_in(stream_key, axis), (), 0, length) for axis, length in enumerate(entries.shape)]
        where[longest] = (where[longest] + shift) % entries.shape[longest]
        spots.append(tuple(where))
    return entries.at[spots[0]].set(low).at[spots[1]].set(largest)


def shard_levels(rng, extent, pieces, least, high):
    gain = 1.0
    for dim, shards_of in pieces:
        heights = jax.random.uniform(jax.random.fold_in(jax.random.fold_in(rng, 6), dim), (shards_of,), jnp.float32, least / len(pieces), high / len(pieces))
        gain = gain * jnp.repeat(jnp.exp(heights), extent[dim] // shards_of).reshape((-1,) + (1,) * (len(extent) - 1 - dim))
    return gain


def noise(rng, dims, scale, bound, cuts=(), kind=jnp.bfloat16):
    entries = jax.random.normal(rng, dims, jnp.float32) * scale
    if len(cuts) > 0:
        entries = shard_levels(rng, dims, cuts, -0.22, 0.18) * entries
    return jnp.clip(entries, min=-bound, max=bound).astype(kind)


def setup_inputs(seed: int = 0, part: int = 0) -> dict:
    streams_of = jax.random.split(jax.random.key(seed), 16)
    part_keys = jax.random.split(jax.random.fold_in(streams_of[15], part), 16)
    return {
        "velocity": noise(part_keys[0], (3, BRICKS, BX, BY, NZ), 1.0, 6.0, ((1, 16),), jnp.float32),
        "stress": noise(part_keys[1], (6, BRICKS, BX, BY, NZ), 1.0, 6.0, ((1, 16),), jnp.float32),
        "memory": noise(part_keys[2], (6, BRICKS, BX, BY, NZ), 0.5, 4.0, ((1, 16),), jnp.float32),
        "lame_lambda": jnp.clip(1.5 + 1.0 * jax.random.uniform(part_keys[3], (BRICKS, BX, BY, NZ), jnp.float32) ** shard_levels(part_keys[3], (BRICKS, BX, BY, NZ), ((0, 16),), -0.2, 0.2), 1.5, 2.5),
        "lame_mu": jnp.clip(0.1 + 0.4 * jax.random.uniform(part_keys[4], (BRICKS, BX, BY, NZ), jnp.float32) ** shard_levels(part_keys[4], (BRICKS, BX, BY, NZ), ((0, 16),), -0.2, 0.2), 0.1, 0.5),
        "buoyancy": jnp.clip(0.7 + 0.3 * jax.random.uniform(part_keys[5], (BRICKS, BX, BY, NZ), jnp.float32) ** shard_levels(part_keys[5], (BRICKS, BX, BY, NZ), ((0, 16),), -0.2, 0.2), 0.7, 1.0),
        "decay": jnp.clip(0.3 + 0.65 * jax.random.uniform(part_keys[6], (BRICKS, BX, BY, NZ), jnp.float32) ** shard_levels(part_keys[6], (BRICKS, BX, BY, NZ), ((0, 16),), -0.2, 0.2), 0.3, 0.95),
        "loss": jnp.clip(0.1 + 0.9 * jax.random.uniform(part_keys[7], (BRICKS, BX, BY, NZ), jnp.float32) ** shard_levels(part_keys[7], (BRICKS, BX, BY, NZ), ((0, 16),), -0.2, 0.2), 0.1, 1.0),
        "tile_lambda": jnp.clip(3.0 + 1.5 * jax.random.uniform(part_keys[8], (TILES, TCELLS), jnp.float32) ** shard_levels(part_keys[8], (TILES, TCELLS), ((0, 16),), -0.2, 0.2), 3.0, 4.5).astype(jnp.bfloat16),
        "tile_mu": jnp.clip(1.0 + 1.0 * jax.random.uniform(part_keys[9], (TILES, TCELLS), jnp.float32) ** shard_levels(part_keys[9], (TILES, TCELLS), ((0, 16),), -0.2, 0.2), 1.0, 2.0).astype(jnp.bfloat16),
        "tile_buoy": jnp.clip(0.3984375 + 0.19921875 * jax.random.uniform(part_keys[10], (TILES, TCELLS), jnp.float32) ** shard_levels(part_keys[10], (TILES, TCELLS), ((0, 16),), -0.2, 0.2), 0.3984375, 0.59765625).astype(jnp.bfloat16),
        "tile_dest": draw_tile_dest(jax.random.fold_in(jax.random.fold_in(streams_of[15], part), 71), part),
        "brick_tiles": draw_brick_tiles(jax.random.fold_in(jax.random.fold_in(streams_of[15], part), 71), part),
        "src_index": place_ends(jax.random.randint(part_keys[13], (ELEMS,), 0, BX * BY * NZ), jax.random.fold_in(part_keys[13], 1), 0, (BX * BY * NZ) - 1).astype(jnp.int32),
        "src_wave": noise(part_keys[14], (ELEMS, STEPS), 1.0, 6.0, ((0, 16),), jnp.float32),
    }


courant = 0.25


def forward_diff(values, along):
    rest = lax.slice_in_dim(values, 1, values.shape[along], axis=along)
    padding = jnp.zeros_like(lax.slice_in_dim(values, 0, 1, axis=along))
    return jnp.concatenate([rest, padding], axis=along) - values


def backward_diff(values, along):
    padding = jnp.zeros_like(lax.slice_in_dim(values, 0, 1, axis=along))
    rest = lax.slice_in_dim(values, 0, values.shape[along] - 1, axis=along)
    return values - jnp.concatenate([padding, rest], axis=along)


def to_grid(values):
    lead = values.shape[:-4]
    shaped = values.reshape(lead + (PX, PY, BX, BY, NZ))
    count = len(lead)
    order = tuple(range(count)) + (count, count + 2, count + 1, count + 3, count + 4)
    return shaped.transpose(order).reshape(lead + (NX, NY, NZ))


def from_grid(values):
    lead = values.shape[:-3]
    shaped = values.reshape(lead + (PX, BX, PY, BY, NZ))
    count = len(lead)
    order = tuple(range(count)) + (count, count + 2, count + 1, count + 3, count + 4)
    return shaped.transpose(order).reshape(lead + (BRICKS, BX, BY, NZ))


def to_helix(grid_field):
    return from_grid(grid_field).transpose(1, 0, 2, 3).reshape(BX, BRICKS * BY, NZ)


def from_helix(cycle_field):
    return to_grid(cycle_field.reshape(BX, BRICKS, BY, NZ).transpose(1, 0, 2, 3))


def helix_forward(values):
    cycle_field = to_helix(values)
    return from_helix(jnp.roll(cycle_field, -1, axis=1) - cycle_field)


def helix_backward(values):
    cycle_field = to_helix(values)
    return from_helix(cycle_field - jnp.roll(cycle_field, 1, axis=1))


def bone_field(background, tiles, brick_tiles, tile_dest):
    safe_ids = jnp.where(brick_tiles >= 0, brick_tiles, 0).astype(jnp.int32)
    owner_ok = jnp.take(tile_dest, safe_ids, axis=0) == jnp.arange(BRICKS, dtype=jnp.int32)[:, None]
    live = (brick_tiles >= 0) & owner_ok
    picked = jnp.take(tiles, safe_ids, axis=0).astype(jnp.float32)
    picked = picked.reshape(BRICKS, SUBS_Y, SUBS_Z, BX, TY, TZ).transpose(0, 3, 1, 4, 2, 5).reshape(BRICKS, BX, BY, NZ)
    inside = jnp.broadcast_to(live.reshape(BRICKS, SUBS_Y, SUBS_Z)[:, None, :, None, :, None], (BRICKS, BX, SUBS_Y, TY, SUBS_Z, TZ)).reshape(BRICKS, BX, BY, NZ)
    return to_grid(jnp.where(inside, picked, background))


def reference(velocity, stress, memory, lame_lambda, lame_mu, buoyancy, decay, loss, tile_lambda, tile_mu, tile_buoy, tile_dest, brick_tiles, src_index, src_wave):
    lame = bone_field(lame_lambda, tile_lambda, brick_tiles, tile_dest)
    shear = bone_field(lame_mu, tile_mu, brick_tiles, tile_dest)
    buoy_field = bone_field(buoyancy, tile_buoy, brick_tiles, tile_dest)
    decay_grid = to_grid(decay)
    loss_grid = to_grid(loss)
    velocity = to_grid(velocity)
    stress = to_grid(stress)
    memory = to_grid(memory)
    owners = jnp.arange(ELEMS, dtype=jnp.int32) // ELEMS_DEV
    cells = owners * (BX * BY * NZ) + src_index
    for step_index in range(STEPS):
        grad_x = forward_diff(stress[0], 0) + helix_backward(stress[3]) + backward_diff(stress[4], 2)
        grad_y = backward_diff(stress[3], 0) + helix_forward(stress[1]) + backward_diff(stress[5], 2)
        grad_z = backward_diff(stress[4], 0) + helix_backward(stress[5]) + forward_diff(stress[2], 2)
        velocity = velocity + courant * buoy_field * jnp.stack([grad_x, grad_y, grad_z])
        strain_x = backward_diff(velocity[0], 0)
        strain_y = helix_backward(velocity[1])
        strain_z = backward_diff(velocity[2], 2)
        dilation = strain_x + strain_y + strain_z
        rates = jnp.stack([
            lame * dilation + 2.0 * shear * strain_x,
            lame * dilation + 2.0 * shear * strain_y,
            lame * dilation + 2.0 * shear * strain_z,
            shear * (helix_forward(velocity[0]) + forward_diff(velocity[1], 0)),
            shear * (forward_diff(velocity[0], 2) + forward_diff(velocity[2], 0)),
            shear * (forward_diff(velocity[1], 2) + helix_forward(velocity[2]))])
        memory = decay_grid * memory - (1.0 - decay_grid) * loss_grid * rates
        stress = stress + courant * (rates + memory)
        source = jnp.zeros((BRICKS * BX * BY * NZ,), jnp.float32).at[cells].add(src_wave[:, step_index]).reshape(BRICKS, BX, BY, NZ)
        stress = stress.at[:3].add(to_grid(source)[None])
    return from_grid(velocity), from_grid(stress), from_grid(memory)
```

```python
import functools

import jax
import jax.numpy as jnp
from jax import lax
from jax.experimental import pallas as pl
from jax.experimental.pallas import tpu as pltpu
from jax.sharding import PartitionSpec as P

MESH = pl.DeviceIdType.MESH
F32 = jnp.float32
PY = 8
TY = 8
TZ = 8
COURANT = 0.25
UNROLL = 16


def each(count, body):
    if count <= UNROLL:
        for k in range(count):
            body(k)
    else:
        lax.fori_loop(0, count, lambda k, c: (body(k), c)[1], 0)


def kernel(
    n, steps,
    vel, stress, mem, lam, mu, buo, dec, los,
    tile_l, tile_m, tile_b, dest, bricks, index, wave,
    out_v, out_s, out_m,
    V, S, M, LAM, MU, BUO, DEC, LOS,
    packed, arrived, source,
    xa_send, xa_recv, xb_recv, ya_send, ya_recv, yb_send, yb_recv,
    load_sem, store_sem, tile_send, tile_recv, send_sem, recv_sem,
):
    me = lax.axis_index("gx")
    nx, ny, nz = LAM.shape
    per_device = tile_l.shape[0]
    has_ahead = me + PY < n
    has_behind = me >= PY
    next_y = lax.rem(me + 1, n)
    prev_y = lax.rem(me + n - 1, n)

    barrier = pltpu.get_barrier_semaphore()

    def greet(k):
        pl.semaphore_signal(
            barrier, inc=1, device_id={"gx": lax.rem(me + 1 + k, n)}, device_id_type=MESH
        )

    each(n - 1, greet)

    loads = [
        pltpu.make_async_copy(stress.at[:, 0], S.at[0], load_sem.at[0]),
        pltpu.make_async_copy(buo.at[0], BUO, load_sem.at[1]),
        pltpu.make_async_copy(vel.at[:, 0], V.at[0], load_sem.at[2]),
        pltpu.make_async_copy(lam.at[0], LAM, load_sem.at[3]),
        pltpu.make_async_copy(mu.at[0], MU, load_sem.at[4]),
        pltpu.make_async_copy(dec.at[0], DEC, load_sem.at[5]),
        pltpu.make_async_copy(los.at[0], LOS, load_sem.at[6]),
        pltpu.make_async_copy(mem.at[:, 0], M, load_sem.at[7]),
    ]
    for load in loads:
        load.start()

    rows = n * TZ
    row = lax.broadcasted_iota(jnp.int32, (rows, per_device), 0)
    chosen = (dest[...] == row // TZ).astype(F32)
    cells = tile_l.shape[1]
    wide_row = lax.broadcasted_iota(jnp.int32, (rows, cells), 0)
    wide_lane = lax.broadcasted_iota(jnp.int32, (rows, cells), 1)
    same = wide_row % TZ == wide_lane % TZ
    fold_row = lax.broadcasted_iota(jnp.int32, (cells, 128), 0) // TZ
    fold_lane = lax.broadcasted_iota(jnp.int32, (cells, 128), 1)
    total = jnp.zeros((rows, 128), F32)
    for prop, tiles in enumerate((tile_l, tile_m, tile_b)):
        spread = jnp.dot(chosen, tiles[...].astype(F32), preferred_element_type=F32)
        spread = jnp.where(same, spread, 0.0)
        fold = (fold_lane == fold_row + prop * nx * TY).astype(F32)
        total = total + jnp.dot(spread, fold, preferred_element_type=F32)
    packed[...] = total
    here = pl.ds(pl.multiple_of(me * TZ, TZ), TZ)
    arrived[here, :] = packed[here, :]

    @pl.when(jnp.logical_not(has_ahead))
    def _():
        xa_recv[...] = jnp.zeros_like(xa_recv)

    @pl.when(jnp.logical_not(has_behind))
    def _():
        xb_recv[...] = jnp.zeros_like(xb_recv)

    def copy_xa(r):
        count = 1 + r % 2
        return pltpu.make_async_remote_copy(
            xa_send.at[r, pl.ds(0, count)], xa_recv.at[r, pl.ds(0, count)],
            send_sem.at[r * 4], recv_sem.at[r * 4],
            device_id={"gx": lax.rem(me + n - PY, n)}, device_id_type=MESH,
        )

    def copy_xb(r):
        count = 2 - r % 2
        if r % 2 == 0:
            src = S.at[r // 2, pl.ds(3, 2), nx - 1]
        else:
            src = V.at[r // 2 + 1, pl.ds(0, 1), nx - 1]
        return pltpu.make_async_remote_copy(
            src, xb_recv.at[r, pl.ds(0, count)],
            send_sem.at[r * 4 + 1], recv_sem.at[r * 4 + 1],
            device_id={"gx": lax.rem(me + PY, n)}, device_id_type=MESH,
        )

    def copy_ya(r):
        return pltpu.make_async_remote_copy(
            ya_send.at[r], ya_recv.at[r], send_sem.at[r * 4 + 2], recv_sem.at[r * 4 + 2],
            device_id={"gx": prev_y}, device_id_type=MESH,
        )

    def copy_yb(r):
        return pltpu.make_async_remote_copy(
            yb_send.at[r], yb_recv.at[r], send_sem.at[r * 4 + 3], recv_sem.at[r * 4 + 3],
            device_id={"gx": next_y}, device_id_type=MESH,
        )

    def send_x_first(r, planes):
        for c, plane in enumerate(planes):
            xa_send[r, c] = plane.astype(jnp.bfloat16)
        pl.when(has_behind)(lambda: copy_xa(r).start())

    def send_x_last(r):
        pl.when(has_ahead)(lambda: copy_xb(r).start())

    def send_y(r, first, last):
        for c, (ref, comp) in enumerate(first):
            ya_send[r, c * nx:(c + 1) * nx, :] = ref[comp, :, 0, :]
        if len(first) == 1:
            ya_send[r, nx:, :] = jnp.zeros((8 - nx, nz), F32)
        for c, (ref, comp) in enumerate(last):
            yb_send[r, c * nx:(c + 1) * nx, :] = ref[comp, :, ny - 1, :]
        if len(last) == 1:
            yb_send[r, nx:, :] = jnp.zeros((8 - nx, nz), F32)
        copy_ya(r).start()
        copy_yb(r).start()

    def receive(r):
        copy_ya(r).wait_recv()
        copy_yb(r).wait_recv()
        pl.when(has_ahead)(lambda: copy_xa(r).wait_recv())
        pl.when(has_behind)(lambda: copy_xb(r).wait_recv())

    elems = index.shape[1]
    cell = index[...]
    where_row = (cell // nz).astype(F32)
    where_lane = (cell % nz).astype(F32)
    eye = lax.broadcasted_iota(jnp.int32, (elems, elems), 0) == lax.broadcasted_iota(
        jnp.int32, (elems, elems), 1
    )
    lane_of = jnp.sum(jnp.where(eye, where_lane, 0.0), axis=1, keepdims=True)
    on_row = (
        lax.broadcasted_iota(jnp.int32, (nx * ny, elems), 0).astype(F32) == where_row
    ).astype(F32)
    on_lane = lax.broadcasted_iota(jnp.int32, (elems, nz), 1).astype(F32) == lane_of
    for step in range(steps):
        amounts = jnp.where(on_lane, wave[:, step:step + 1], 0.0)
        source[step] = jnp.dot(
            on_row, amounts, preferred_element_type=F32, precision=lax.Precision.HIGHEST
        ).reshape(nx, ny, nz)

    spots = bricks.shape[1]
    width = spots * TZ
    owner = jnp.floor((bricks[...].astype(F32) + 0.5) * (1.0 / per_device))
    expand = (
        lax.broadcasted_iota(jnp.int32, (spots, width), 0)
        == lax.broadcasted_iota(jnp.int32, (spots, width), 1) // TZ
    ).astype(F32)
    owners = jnp.dot(
        jnp.broadcast_to(owner, (8, spots)), expand, preferred_element_type=F32
    )[0:1]
    live = owners >= 0.0
    place_row = lax.broadcasted_iota(jnp.int32, (rows, width), 0)
    place_lane = lax.broadcasted_iota(jnp.int32, (rows, width), 1)
    spread_to = (
        ((place_row // TZ).astype(F32) == owners) & (place_row % TZ == place_lane % TZ)
    ).astype(F32)

    loads[0].wait()
    pl.semaphore_wait(barrier, n - 1)

    send_x_last(0)
    send_x_first(0, [S[0, 0, 0]])

    def send_tiles(k):
        target = lax.rem(me + 1 + k, n)
        there = pl.ds(pl.multiple_of(target * TZ, TZ), TZ)
        pltpu.make_async_remote_copy(
            packed.at[there], arrived.at[here], tile_send, tile_recv,
            device_id={"gx": target}, device_id_type=MESH,
        ).start()

    each(n - 1, send_tiles)
    send_y(0, [(S.at[0], 1)], [(S.at[0], 3), (S.at[0], 5)])

    for load in loads[1:]:
        load.wait()

    part = pl.ds(0, (n - 1) * TZ)
    pltpu.make_async_copy(arrived.at[part], arrived.at[part], tile_recv).wait()
    placed = lax.dot_general(
        arrived[...].T, spread_to, (((1,), (0,)), ((), ())), preferred_element_type=F32
    )
    for prop, field in enumerate((LAM, MU, BUO)):
        for i in range(nx):
            for ry in range(ny // TY):
                top = (prop * nx + i) * TY
                piece = placed[top:top + TY, ry * nz:(ry + 1) * nz]
                at = slice(ry * TY, (ry + 1) * TY)
                field[i, at, :] = jnp.where(
                    live[:, ry * nz:(ry + 1) * nz], piece, field[i, at, :]
                )

    y_of = lax.broadcasted_iota(jnp.int32, (ny, nz), 0)
    z_of = lax.broadcasted_iota(jnp.int32, (ny, nz), 1)

    def after_y(a, halo):
        return jnp.where(y_of == ny - 1, halo, pltpu.roll(a, ny - 1, 0))

    def before_y(a, halo):
        return jnp.where(y_of == 0, halo, pltpu.roll(a, 1, 0))

    def after_z(a):
        return jnp.where(z_of == nz - 1, 0.0, pltpu.roll(a, nz - 1, 1))

    def before_z(a):
        return jnp.where(z_of == 0, 0.0, pltpu.roll(a, 1, 1))

    order = [0, nx - 1] + list(range(1, nx - 1))
    stores = []

    for step in range(steps):
        last = step == steps - 1
        r = 2 * step
        s, v_old, v = S.at[step], V.at[step], V.at[step + 1]
        receive(r)

        def row_of(buf, r, comp, i):
            at = comp * nx + i
            return buf[r, at:at + 1, :]

        for i in order:
            scale = COURANT * BUO[i]
            xy, xz, yz = s[3, i], s[4, i], s[5, i]
            ahead = s[0, i + 1] if i < nx - 1 else xa_recv[r, 0].astype(F32)
            gx = (
                (ahead - s[0, i])
                + (xy - before_y(xy, row_of(yb_recv, r, 0, i)))
                + (xz - before_z(xz))
            )
            behind = s[3, i - 1] if i > 0 else xb_recv[r, 0]
            yy = s[1, i]
            gy = (
                (xy - behind)
                + (after_y(yy, row_of(ya_recv, r, 0, i)) - yy)
                + (yz - before_z(yz))
            )
            behind = s[4, i - 1] if i > 0 else xb_recv[r, 1]
            zz = s[2, i]
            gz = (
                (xz - behind)
                + (yz - before_y(yz, row_of(yb_recv, r, 1, i)))
                + (after_z(zz) - zz)
            )
            v[0, i] = v_old[0, i] + scale * gx
            v[1, i] = v_old[1, i] + scale * gy
            v[2, i] = v_old[2, i] + scale * gz
            if i == 0:
                send_x_first(r + 1, [v[1, 0], v[2, 0]])
            if i == nx - 1:
                send_x_last(r + 1)
        send_y(r + 1, [(v, 0), (v, 2)], [(v, 1)])
        if last:
            stores.append(pltpu.make_async_copy(v, out_v.at[:, 0], store_sem.at[0]))
            stores[-1].start()

        r = r + 1
        receive(r)
        s_new = S.at[step + 1]
        for i in order:
            lame, shear = LAM[i], MU[i]
            vx, vy, vz = v[0, i], v[1, i], v[2, i]
            behind = v[0, i - 1] if i > 0 else xb_recv[r, 0]
            ex = vx - behind
            ey = vy - before_y(vy, row_of(yb_recv, r, 0, i))
            ez = vz - before_z(vz)
            spread = lame * (ex + ey + ez)
            ahead_y = v[1, i + 1] if i < nx - 1 else xa_recv[r, 0].astype(F32)
            ahead_z = v[2, i + 1] if i < nx - 1 else xa_recv[r, 1].astype(F32)
            rates = (
                spread + 2.0 * shear * ex,
                spread + 2.0 * shear * ey,
                spread + 2.0 * shear * ez,
                shear * ((after_y(vx, row_of(ya_recv, r, 0, i)) - vx) + (ahead_y - vy)),
                shear * ((after_z(vx) - vx) + (ahead_z - vz)),
                shear * ((after_z(vy) - vy) + (after_y(vz, row_of(ya_recv, r, 1, i)) - vz)),
            )
            keep = DEC[i]
            drop = (1.0 - keep) * LOS[i]
            for c in range(6):
                m = keep * M[c, i] - drop * rates[c]
                M[c, i] = m
                new = s[c, i] + COURANT * (rates[c] + m)
                s_new[c, i] = new + source[step, i] if c < 3 else new
            if last:
                k = 1 + 2 * i
                stores.append(
                    pltpu.make_async_copy(s_new.at[:, i], out_s.at[:, 0, i], store_sem.at[k])
                )
                stores[-1].start()
                stores.append(
                    pltpu.make_async_copy(M.at[:, i], out_m.at[:, 0, i], store_sem.at[k + 1])
                )
                stores[-1].start()
            else:
                if i == 0:
                    send_x_first(r + 1, [s_new[0, 0]])
                if i == nx - 1:
                    send_x_last(r + 1)
        if not last:
            send_y(r + 1, [(s_new, 1)], [(s_new, 3), (s_new, 5)])

    pltpu.make_async_copy(packed.at[part], packed.at[part], tile_send).wait()
    for r in range(2 * steps):
        copy_ya(r).wait_send()
        copy_yb(r).wait_send()
        pl.when(has_behind)(functools.partial(lambda q: copy_xa(q).wait_send(), r))
        pl.when(has_ahead)(functools.partial(lambda q: copy_xb(q).wait_send(), r))
    for store in stores:
        store.wait()


def body(n, velocity, stress, memory, lame_lambda, lame_mu, buoyancy, decay, loss,
         tile_lambda, tile_mu, tile_buoy, tile_dest, brick_tiles, src_index, src_wave):
    steps = src_wave.shape[1]
    grid = lame_lambda.shape[1:]
    nx, ny, nz = grid
    rounds = 2 * steps
    hbm = pl.BlockSpec(memory_space=pl.ANY)
    vmem = pl.BlockSpec(memory_space=pltpu.VMEM)
    big = (velocity, stress, memory, lame_lambda, lame_mu, buoyancy, decay, loss)
    return pl.pallas_call(
        functools.partial(kernel, n, steps),
        out_shape=tuple(
            jax.ShapeDtypeStruct(a.shape, F32) for a in (velocity, stress, memory)
        ),
        in_specs=[hbm] * len(big) + [vmem] * 7,
        out_specs=(hbm,) * 3,
        scratch_shapes=[
            pltpu.VMEM((steps + 1, 3) + grid, F32),
            pltpu.VMEM((steps + 1, 6) + grid, F32),
            pltpu.VMEM((6,) + grid, F32),
        ] + [pltpu.VMEM(grid, F32)] * 5 + [
            pltpu.VMEM((n * TZ, 128), F32),
            pltpu.VMEM((n * TZ, 128), F32),
            pltpu.VMEM((steps,) + grid, F32),
            pltpu.VMEM((rounds, 2, ny, nz), jnp.bfloat16),
            pltpu.VMEM((rounds, 2, ny, nz), jnp.bfloat16),
            pltpu.VMEM((rounds, 2, ny, nz), F32),
            pltpu.VMEM((rounds, 8, nz), F32),
            pltpu.VMEM((rounds, 8, nz), F32),
            pltpu.VMEM((rounds, 8, nz), F32),
            pltpu.VMEM((rounds, 8, nz), F32),
            pltpu.SemaphoreType.DMA((8,)),
            pltpu.SemaphoreType.DMA((1 + 2 * nx,)),
            pltpu.SemaphoreType.DMA,
            pltpu.SemaphoreType.DMA,
            pltpu.SemaphoreType.DMA((4 * rounds,)),
            pltpu.SemaphoreType.DMA((4 * rounds,)),
        ],
        compiler_params=pltpu.CompilerParams(
            collective_id=0, has_side_effects=True, vmem_limit_bytes=48 * 1024 * 1024
        ),
    )(
        *big, tile_lambda, tile_mu, tile_buoy, tile_dest.reshape(1, -1), brick_tiles,
        src_index.reshape(1, -1), src_wave,
    )


def solution(mesh):
    both = ("groups", "gx")
    field = P(None, both, None, None, None)
    single = P(both, None, None, None)
    return jax.shard_map(
        functools.partial(body, mesh.shape["gx"]),
        mesh=mesh,
        in_specs=(field,) * 3 + (single,) * 5 + (P(both, None),) * 3
        + (P(both), P(both, None), P(both), P(both, None)),
        out_specs=(field,) * 3,
        check_vma=False,
    )
```

```python
import functools

import jax
import jax.numpy as jnp
from jax import lax
from jax.experimental import pallas as pl
from jax.experimental.pallas import tpu as pltpu
from jax.sharding import PartitionSpec as P

MESH = pl.DeviceIdType.MESH
F32 = jnp.float32
PY = 8
TY = 8
TZ = 8
COURANT = 0.25
UNROLL = 16
VMEM_LIMIT = 64 * 1024 * 1024 - 1024 * 1024


def each(count, body):
    if count <= UNROLL:
        for k in range(count):
            body(k)
    else:
        lax.fori_loop(0, count, lambda k, c: (body(k), c)[1], 0)


def kernel(
    n, steps,
    vel, stress, mem, lam, mu, buo, dec, los,
    tile_l_in, tile_m_in, tile_b_in, dest_in, bricks_in, index_in, wave_in,
    last_v, last_s, last_m,
    V, S, M, LAM, MU, BUO, DEC, LOS,
    tile_l, tile_m, tile_b, dest, bricks, index, wave,
    packed, arrived, source,
    xa_send, xa_recv, xb_recv, ya_send, ya_recv, yb_send, yb_recv,
    load_sem, small_sem, tile_send, tile_recv, send_sem, recv_sem,
):
    me = lax.axis_index("gx")
    nx, ny, nz = LAM.shape
    per_device = tile_l.shape[0]
    has_ahead = me + PY < n
    has_behind = me >= PY
    next_y = lax.rem(me + 1, n)
    prev_y = lax.rem(me + n - 1, n)

    barrier = pltpu.get_barrier_semaphore()

    def greet(k):
        pl.semaphore_signal(
            barrier, inc=1, device_id={"gx": lax.rem(me + 1 + k, n)}, device_id_type=MESH
        )

    each(n - 1, greet)

    small = [
        pltpu.make_async_copy(src, dst, small_sem.at[k])
        for k, (src, dst) in enumerate((
            (dest_in, dest), (tile_l_in, tile_l), (tile_m_in, tile_m), (tile_b_in, tile_b),
            (bricks_in, bricks), (index_in, index), (wave_in, wave),
        ))
    ]
    for load in small:
        load.start()
    loads = [
        pltpu.make_async_copy(stress.at[:, 0], S.at[0], load_sem.at[0]),
        pltpu.make_async_copy(buo.at[0], BUO, load_sem.at[1]),
        pltpu.make_async_copy(vel.at[:, 0], V.at[0], load_sem.at[2]),
        pltpu.make_async_copy(lam.at[0], LAM, load_sem.at[3]),
        pltpu.make_async_copy(mu.at[0], MU, load_sem.at[4]),
        pltpu.make_async_copy(dec.at[0], DEC, load_sem.at[5]),
        pltpu.make_async_copy(los.at[0], LOS, load_sem.at[6]),
        pltpu.make_async_copy(mem.at[:, 0], M, load_sem.at[7]),
    ]
    for load in loads:
        load.start()

    for load in small:
        load.wait()

    rows = n * TZ
    row = lax.broadcasted_iota(jnp.int32, (rows, per_device), 0)
    chosen = (dest[...] == row // TZ).astype(F32)
    cells = tile_l.shape[1]
    wide_row = lax.broadcasted_iota(jnp.int32, (rows, cells), 0)
    wide_lane = lax.broadcasted_iota(jnp.int32, (rows, cells), 1)
    same = wide_row % TZ == wide_lane % TZ
    fold_row = lax.broadcasted_iota(jnp.int32, (cells, 128), 0) // TZ
    fold_lane = lax.broadcasted_iota(jnp.int32, (cells, 128), 1)
    total = jnp.zeros((rows, 128), F32)
    for prop, tiles in enumerate((tile_l, tile_m, tile_b)):
        spread = jnp.dot(chosen, tiles[...].astype(F32), preferred_element_type=F32)
        spread = jnp.where(same, spread, 0.0)
        fold = (fold_lane == fold_row + prop * nx * TY).astype(F32)
        total = total + jnp.dot(spread, fold, preferred_element_type=F32)
    packed[...] = total
    here = pl.ds(pl.multiple_of(me * TZ, TZ), TZ)
    arrived[here, :] = packed[here, :]

    @pl.when(jnp.logical_not(has_ahead))
    def _():
        xa_recv[...] = jnp.zeros_like(xa_recv)

    @pl.when(jnp.logical_not(has_behind))
    def _():
        xb_recv[...] = jnp.zeros_like(xb_recv)

    def copy_xa(r):
        count = 1 + r % 2
        return pltpu.make_async_remote_copy(
            xa_send.at[r, pl.ds(0, count)], xa_recv.at[r, pl.ds(0, count)],
            send_sem.at[r * 4], recv_sem.at[r * 4],
            device_id={"gx": lax.rem(me + n - PY, n)}, device_id_type=MESH,
        )

    def copy_xb(r):
        count = 2 - r % 2
        if r % 2 == 0:
            src = S.at[r // 2, pl.ds(3, 2), nx - 1]
        else:
            v = last_v if r // 2 == steps - 1 else V.at[r // 2 + 1]
            src = v.at[pl.ds(0, 1), nx - 1]
        return pltpu.make_async_remote_copy(
            src, xb_recv.at[r, pl.ds(0, count)],
            send_sem.at[r * 4 + 1], recv_sem.at[r * 4 + 1],
            device_id={"gx": lax.rem(me + PY, n)}, device_id_type=MESH,
        )

    def copy_ya(r):
        return pltpu.make_async_remote_copy(
            ya_send.at[r], ya_recv.at[r], send_sem.at[r * 4 + 2], recv_sem.at[r * 4 + 2],
            device_id={"gx": prev_y}, device_id_type=MESH,
        )

    def copy_yb(r):
        return pltpu.make_async_remote_copy(
            yb_send.at[r], yb_recv.at[r], send_sem.at[r * 4 + 3], recv_sem.at[r * 4 + 3],
            device_id={"gx": next_y}, device_id_type=MESH,
        )

    def send_x_first(r, planes):
        for c, plane in enumerate(planes):
            xa_send[r, c] = plane.astype(jnp.bfloat16)
        pl.when(has_behind)(lambda: copy_xa(r).start())

    def send_x_last(r):
        pl.when(has_ahead)(lambda: copy_xb(r).start())

    def send_y(r, first, last):
        for c, (ref, comp) in enumerate(first):
            ya_send[r, c * nx:(c + 1) * nx, :] = ref[comp, :, 0, :]
        if len(first) == 1:
            ya_send[r, nx:, :] = jnp.zeros((8 - nx, nz), F32)
        for c, (ref, comp) in enumerate(last):
            yb_send[r, c * nx:(c + 1) * nx, :] = ref[comp, :, ny - 1, :]
        if len(last) == 1:
            yb_send[r, nx:, :] = jnp.zeros((8 - nx, nz), F32)
        copy_ya(r).start()
        copy_yb(r).start()

    def receive(r):
        copy_ya(r).wait_recv()
        copy_yb(r).wait_recv()
        pl.when(has_ahead)(lambda: copy_xa(r).wait_recv())
        pl.when(has_behind)(lambda: copy_xb(r).wait_recv())

    elems = index.shape[1]
    cell = index[...]
    where_row = (cell // nz).astype(F32)
    where_lane = (cell % nz).astype(F32)
    eye = lax.broadcasted_iota(jnp.int32, (elems, elems), 0) == lax.broadcasted_iota(
        jnp.int32, (elems, elems), 1
    )
    lane_of = jnp.sum(jnp.where(eye, where_lane, 0.0), axis=1, keepdims=True)
    on_row = (
        lax.broadcasted_iota(jnp.int32, (nx * ny, elems), 0).astype(F32) == where_row
    ).astype(F32)
    on_lane = (
        lax.broadcasted_iota(jnp.int32, (elems, nz), 1).astype(F32) == lane_of
    ).astype(F32)
    for step in range(steps):
        amounts = on_row * wave[step:step + 1, :]
        source[step] = jnp.dot(
            amounts, on_lane, preferred_element_type=F32, precision=lax.Precision.HIGHEST
        ).reshape(nx, ny, nz)

    spots = bricks.shape[1]
    width = spots * TZ
    owner = jnp.floor((bricks[...].astype(F32) + 0.5) * (1.0 / per_device))
    expand = (
        lax.broadcasted_iota(jnp.int32, (spots, width), 0)
        == lax.broadcasted_iota(jnp.int32, (spots, width), 1) // TZ
    ).astype(F32)
    owners = jnp.dot(
        jnp.broadcast_to(owner, (8, spots)), expand, preferred_element_type=F32
    )[0:1]
    live = owners >= 0.0
    place_row = lax.broadcasted_iota(jnp.int32, (rows, width), 0)
    place_lane = lax.broadcasted_iota(jnp.int32, (rows, width), 1)
    spread_to = (
        ((place_row // TZ).astype(F32) == owners) & (place_row % TZ == place_lane % TZ)
    ).astype(F32)

    loads[0].wait()
    pl.semaphore_wait(barrier, n - 1)

    send_x_last(0)
    send_x_first(0, [S[0, 0, 0]])

    def send_tiles(k):
        target = lax.rem(me + 1 + k, n)
        there = pl.ds(pl.multiple_of(target * TZ, TZ), TZ)
        pltpu.make_async_remote_copy(
            packed.at[there], arrived.at[here], tile_send, tile_recv,
            device_id={"gx": target}, device_id_type=MESH,
        ).start()

    each(n - 1, send_tiles)
    send_y(0, [(S.at[0], 1)], [(S.at[0], 3), (S.at[0], 5)])

    for load in loads[1:]:
        load.wait()

    part = pl.ds(0, (n - 1) * TZ)
    pltpu.make_async_copy(arrived.at[part], arrived.at[part], tile_recv).wait()
    placed = lax.dot_general(
        arrived[...].T, spread_to, (((1,), (0,)), ((), ())), preferred_element_type=F32
    )
    for prop, field in enumerate((LAM, MU, BUO)):
        for i in range(nx):
            for ry in range(ny // TY):
                top = (prop * nx + i) * TY
                piece = placed[top:top + TY, ry * nz:(ry + 1) * nz]
                at = slice(ry * TY, (ry + 1) * TY)
                field[i, at, :] = jnp.where(
                    live[:, ry * nz:(ry + 1) * nz], piece, field[i, at, :]
                )

    y_of = lax.broadcasted_iota(jnp.int32, (ny, nz), 0)
    z_of = lax.broadcasted_iota(jnp.int32, (ny, nz), 1)

    def after_y(a, halo):
        return jnp.where(y_of == ny - 1, halo, pltpu.roll(a, ny - 1, 0))

    def before_y(a, halo):
        return jnp.where(y_of == 0, halo, pltpu.roll(a, 1, 0))

    def after_z(a):
        return jnp.where(z_of == nz - 1, 0.0, pltpu.roll(a, nz - 1, 1))

    def before_z(a):
        return jnp.where(z_of == 0, 0.0, pltpu.roll(a, 1, 1))

    order = [0, nx - 1] + list(range(1, nx - 1))
    for step in range(steps):
        last = step == steps - 1
        r = 2 * step
        s, v_old = S.at[step], V.at[step]
        v = last_v if last else V.at[step + 1]
        s_new = last_s if last else S.at[step + 1]
        m_new = last_m if last else M
        receive(r)

        def row_of(buf, r, comp, i):
            at = comp * nx + i
            return buf[r, at:at + 1, :]

        for i in order:
            scale = COURANT * BUO[i]
            xy, xz, yz = s[3, i], s[4, i], s[5, i]
            ahead = s[0, i + 1] if i < nx - 1 else xa_recv[r, 0].astype(F32)
            gx = (
                (ahead - s[0, i])
                + (xy - before_y(xy, row_of(yb_recv, r, 0, i)))
                + (xz - before_z(xz))
            )
            behind = s[3, i - 1] if i > 0 else xb_recv[r, 0]
            yy = s[1, i]
            gy = (
                (xy - behind)
                + (after_y(yy, row_of(ya_recv, r, 0, i)) - yy)
                + (yz - before_z(yz))
            )
            behind = s[4, i - 1] if i > 0 else xb_recv[r, 1]
            zz = s[2, i]
            gz = (
                (xz - behind)
                + (yz - before_y(yz, row_of(yb_recv, r, 1, i)))
                + (after_z(zz) - zz)
            )
            v[0, i] = v_old[0, i] + scale * gx
            v[1, i] = v_old[1, i] + scale * gy
            v[2, i] = v_old[2, i] + scale * gz
            if i == 0:
                send_x_first(r + 1, [v[1, 0], v[2, 0]])
            if i == nx - 1:
                send_x_last(r + 1)
        send_y(r + 1, [(v, 0), (v, 2)], [(v, 1)])

        r = r + 1
        receive(r)
        for i in order:
            lame, shear = LAM[i], MU[i]
            vx, vy, vz = v[0, i], v[1, i], v[2, i]
            behind = v[0, i - 1] if i > 0 else xb_recv[r, 0]
            ex = vx - behind
            ey = vy - before_y(vy, row_of(yb_recv, r, 0, i))
            ez = vz - before_z(vz)
            spread = lame * (ex + ey + ez)
            ahead_y = v[1, i + 1] if i < nx - 1 else xa_recv[r, 0].astype(F32)
            ahead_z = v[2, i + 1] if i < nx - 1 else xa_recv[r, 1].astype(F32)
            rates = (
                spread + 2.0 * shear * ex,
                spread + 2.0 * shear * ey,
                spread + 2.0 * shear * ez,
                shear * ((after_y(vx, row_of(ya_recv, r, 0, i)) - vx) + (ahead_y - vy)),
                shear * ((after_z(vx) - vx) + (ahead_z - vz)),
                shear * ((after_z(vy) - vy) + (after_y(vz, row_of(ya_recv, r, 1, i)) - vz)),
            )
            keep = DEC[i]
            drop = (1.0 - keep) * LOS[i]
            for c in range(6):
                m = keep * M[c, i] - drop * rates[c]
                m_new[c, i] = m
                new = s[c, i] + COURANT * (rates[c] + m)
                s_new[c, i] = new + source[step, i] if c < 3 else new
            if not last and i == 0:
                send_x_first(r + 1, [s_new[0, 0]])
            if not last and i == nx - 1:
                send_x_last(r + 1)
        if not last:
            send_y(r + 1, [(s_new, 1)], [(s_new, 3), (s_new, 5)])

    pltpu.make_async_copy(packed.at[part], packed.at[part], tile_send).wait()
    for r in range(2 * steps):
        copy_ya(r).wait_send()
        copy_yb(r).wait_send()
        pl.when(has_behind)(functools.partial(lambda q: copy_xa(q).wait_send(), r))
        pl.when(has_ahead)(functools.partial(lambda q: copy_xb(q).wait_send(), r))


def write(v, s, m, out_v, out_s, out_m, sems):
    stores = [
        pltpu.make_async_copy(src, dst.at[:, 0], sems.at[k])
        for k, (src, dst) in enumerate(((s, out_s), (m, out_m), (v, out_v)))
    ]
    for store in stores:
        store.start()
    for store in stores:
        store.wait()


def body(n, velocity, stress, memory, lame_lambda, lame_mu, buoyancy, decay, loss,
         tile_lambda, tile_mu, tile_buoy, tile_dest, brick_tiles, src_index, src_wave):
    steps = src_wave.shape[1]
    grid = lame_lambda.shape[1:]
    nx, ny, nz = grid
    rounds = 2 * steps
    hbm = pl.BlockSpec(memory_space=pltpu.HBM)
    vmem = pl.BlockSpec(memory_space=pltpu.VMEM)
    big = (velocity, stress, memory, lame_lambda, lame_mu, buoyancy, decay, loss)
    small = (tile_lambda, tile_mu, tile_buoy, tile_dest.reshape(1, -1), brick_tiles,
             src_index.reshape(1, -1), src_wave.T)
    states = pl.pallas_call(
        functools.partial(kernel, n, steps),
        out_shape=tuple(jax.ShapeDtypeStruct((c,) + grid, F32) for c in (3, 6, 6)),
        in_specs=[hbm] * (len(big) + len(small)),
        out_specs=(vmem,) * 3,
        scratch_shapes=[
            pltpu.VMEM((steps, 3) + grid, F32),
            pltpu.VMEM((steps, 6) + grid, F32),
            pltpu.VMEM((6,) + grid, F32),
        ] + [pltpu.VMEM(grid, F32)] * 5 + [pltpu.VMEM(a.shape, a.dtype) for a in small] + [
            pltpu.VMEM((n * TZ, 128), F32),
            pltpu.VMEM((n * TZ, 128), F32),
            pltpu.VMEM((steps,) + grid, F32),
            pltpu.VMEM((rounds, 2, ny, nz), jnp.bfloat16),
            pltpu.VMEM((rounds, 2, ny, nz), jnp.bfloat16),
            pltpu.VMEM((rounds, 2, ny, nz), F32),
            pltpu.VMEM((rounds, 8, nz), F32),
            pltpu.VMEM((rounds, 8, nz), F32),
            pltpu.VMEM((rounds, 8, nz), F32),
            pltpu.VMEM((rounds, 8, nz), F32),
            pltpu.SemaphoreType.DMA((8,)),
            pltpu.SemaphoreType.DMA((len(small),)),
            pltpu.SemaphoreType.DMA,
            pltpu.SemaphoreType.DMA,
            pltpu.SemaphoreType.DMA((4 * rounds,)),
            pltpu.SemaphoreType.DMA((4 * rounds,)),
        ],
        compiler_params=pltpu.CompilerParams(
            collective_id=0, has_side_effects=True, vmem_limit_bytes=VMEM_LIMIT
        ),
    )(*big, *small)
    return pl.pallas_call(
        write,
        out_shape=tuple(
            jax.ShapeDtypeStruct(a.shape, F32) for a in (velocity, stress, memory)
        ),
        in_specs=[pl.BlockSpec(memory_space=pl.ANY)] * 3,
        out_specs=(hbm,) * 3,
        scratch_shapes=[pltpu.SemaphoreType.DMA((3,))],
    )(*states)


def solution(mesh):
    both = ("groups", "gx")
    field = P(None, both, None, None, None)
    single = P(both, None, None, None)
    return jax.shard_map(
        functools.partial(body, mesh.shape["gx"]),
        mesh=mesh,
        in_specs=(field,) * 3 + (single,) * 5 + (P(both, None),) * 3
        + (P(both), P(both, None), P(both), P(both, None)),
        out_specs=(field,) * 3,
        check_vma=False,
    )
```

```python
import functools

import jax
import jax.numpy as jnp
from jax import lax
from jax.experimental import pallas as pl
from jax.experimental.pallas import tpu as pltpu
from jax.sharding import PartitionSpec as P

MESH = pl.DeviceIdType.MESH
F32 = jnp.float32
PY = 8
TY = 8
TZ = 8
COURANT = 0.25
UNROLL = 16
VMEM_LIMIT = 64 * 1024 * 1024 - 1024 * 1024


def each(count, body):
    if count <= UNROLL:
        for k in range(count):
            body(k)
    else:
        lax.fori_loop(0, count, lambda k, c: (body(k), c)[1], 0)


def kernel(
    n, steps,
    vel, stress, mem, lam, mu, buo, dec, los,
    tile_l_in, tile_m_in, tile_b_in, dest_in, bricks_in, index_in, wave_in,
    last_v, last_s, last_m,
    V, S, M, LAM, MU, BUO, DEC, LOS,
    tile_l, tile_m, tile_b, dest, bricks, index, wave,
    packed, arrived, source,
    xa_send, xa_recv, xb_recv, ya_send, ya_recv, yb_send, yb_recv,
    load_sem, small_sem, tile_send, tile_recv, send_sem, recv_sem,
):
    me = lax.axis_index("gx")
    nx, ny, nz = LAM.shape
    per_device = tile_l.shape[0]
    has_ahead = me + PY < n
    has_behind = me >= PY
    next_y = lax.rem(me + 1, n)
    prev_y = lax.rem(me + n - 1, n)

    barrier = pltpu.get_barrier_semaphore()

    def greet(k):
        pl.semaphore_signal(
            barrier, inc=1, device_id={"gx": lax.rem(me + 1 + k, n)}, device_id_type=MESH
        )

    each(n - 1, greet)

    small = [
        pltpu.make_async_copy(src, dst, small_sem.at[k])
        for k, (src, dst) in enumerate((
            (dest_in, dest), (tile_l_in, tile_l), (tile_m_in, tile_m), (tile_b_in, tile_b),
            (bricks_in, bricks), (index_in, index), (wave_in, wave),
        ))
    ]
    for load in small:
        load.start()
    loads = [
        pltpu.make_async_copy(stress.at[:, 0], S.at[0], load_sem.at[0]),
        pltpu.make_async_copy(buo.at[0], BUO, load_sem.at[1]),
        pltpu.make_async_copy(vel.at[:, 0], V.at[0], load_sem.at[2]),
        pltpu.make_async_copy(lam.at[0], LAM, load_sem.at[3]),
        pltpu.make_async_copy(mu.at[0], MU, load_sem.at[4]),
        pltpu.make_async_copy(dec.at[0], DEC, load_sem.at[5]),
        pltpu.make_async_copy(los.at[0], LOS, load_sem.at[6]),
        pltpu.make_async_copy(mem.at[:, 0], M, load_sem.at[7]),
    ]
    for load in loads:
        load.start()

    for load in small:
        load.wait()

    rows = n * TZ
    row = lax.broadcasted_iota(jnp.int32, (rows, per_device), 0)
    chosen = (dest[...] == row // TZ).astype(F32)
    cells = tile_l.shape[1]
    wide_row = lax.broadcasted_iota(jnp.int32, (rows, cells), 0)
    wide_lane = lax.broadcasted_iota(jnp.int32, (rows, cells), 1)
    same = wide_row % TZ == wide_lane % TZ
    fold_row = lax.broadcasted_iota(jnp.int32, (cells, 128), 0) // TZ
    fold_lane = lax.broadcasted_iota(jnp.int32, (cells, 128), 1)
    total = jnp.zeros((rows, 128), F32)
    for prop, tiles in enumerate((tile_l, tile_m, tile_b)):
        spread = jnp.dot(chosen, tiles[...].astype(F32), preferred_element_type=F32)
        spread = jnp.where(same, spread, 0.0)
        fold = (fold_lane == fold_row + prop * nx * TY).astype(F32)
        total = total + jnp.dot(spread, fold, preferred_element_type=F32)
    packed[...] = total
    here = pl.ds(pl.multiple_of(me * TZ, TZ), TZ)
    arrived[here, :] = packed[here, :]

    @pl.when(jnp.logical_not(has_ahead))
    def _():
        xa_recv[...] = jnp.zeros_like(xa_recv)

    @pl.when(jnp.logical_not(has_behind))
    def _():
        xb_recv[...] = jnp.zeros_like(xb_recv)

    def copy_xa(r):
        count = 1 + r % 2
        return pltpu.make_async_remote_copy(
            xa_send.at[r, pl.ds(0, count)], xa_recv.at[r, pl.ds(0, count)],
            send_sem.at[r * 4], recv_sem.at[r * 4],
            device_id={"gx": lax.rem(me + n - PY, n)}, device_id_type=MESH,
        )

    def copy_xb(r):
        count = 2 - r % 2
        if r % 2 == 0:
            src = S.at[r // 2, pl.ds(3, 2), nx - 1]
        else:
            v = last_v if r // 2 == steps - 1 else V.at[r // 2 + 1]
            src = v.at[pl.ds(0, 1), nx - 1]
        return pltpu.make_async_remote_copy(
            src, xb_recv.at[r, pl.ds(0, count)],
            send_sem.at[r * 4 + 1], recv_sem.at[r * 4 + 1],
            device_id={"gx": lax.rem(me + PY, n)}, device_id_type=MESH,
        )

    def copy_ya(r):
        return pltpu.make_async_remote_copy(
            ya_send.at[r], ya_recv.at[r], send_sem.at[r * 4 + 2], recv_sem.at[r * 4 + 2],
            device_id={"gx": prev_y}, device_id_type=MESH,
        )

    def copy_yb(r):
        return pltpu.make_async_remote_copy(
            yb_send.at[r], yb_recv.at[r], send_sem.at[r * 4 + 3], recv_sem.at[r * 4 + 3],
            device_id={"gx": next_y}, device_id_type=MESH,
        )

    def send_x_first(r, planes):
        for c, plane in enumerate(planes):
            xa_send[r, c] = plane.astype(jnp.bfloat16)
        pl.when(has_behind)(lambda: copy_xa(r).start())

    def send_x_last(r):
        pl.when(has_ahead)(lambda: copy_xb(r).start())

    def send_y(r, first, last):
        for c, (ref, comp) in enumerate(first):
            ya_send[r, c * nx:(c + 1) * nx, :] = ref[comp, :, 0, :]
        if len(first) == 1:
            ya_send[r, nx:, :] = jnp.zeros((8 - nx, nz), F32)
        for c, (ref, comp) in enumerate(last):
            yb_send[r, c * nx:(c + 1) * nx, :] = ref[comp, :, ny - 1, :]
        if len(last) == 1:
            yb_send[r, nx:, :] = jnp.zeros((8 - nx, nz), F32)
        copy_ya(r).start()
        copy_yb(r).start()

    def receive(r):
        copy_ya(r).wait_recv()
        copy_yb(r).wait_recv()
        pl.when(has_ahead)(lambda: copy_xa(r).wait_recv())
        pl.when(has_behind)(lambda: copy_xb(r).wait_recv())

    elems = index.shape[1]
    cell = index[...]
    where_row = (cell // nz).astype(F32)
    where_lane = (cell % nz).astype(F32)
    eye = lax.broadcasted_iota(jnp.int32, (elems, elems), 0) == lax.broadcasted_iota(
        jnp.int32, (elems, elems), 1
    )
    lane_of = jnp.sum(jnp.where(eye, where_lane, 0.0), axis=1, keepdims=True)
    on_row = (
        lax.broadcasted_iota(jnp.int32, (nx * ny, elems), 0).astype(F32) == where_row
    ).astype(F32)
    on_lane = (
        lax.broadcasted_iota(jnp.int32, (elems, nz), 1).astype(F32) == lane_of
    ).astype(F32)
    for step in range(steps):
        amounts = on_row * wave[step:step + 1, :]
        source[step] = jnp.dot(
            amounts, on_lane, preferred_element_type=F32, precision=lax.Precision.HIGHEST
        ).reshape(nx, ny, nz)

    spots = bricks.shape[1]
    width = spots * TZ
    owner = jnp.floor((bricks[...].astype(F32) + 0.5) * (1.0 / per_device))
    expand = (
        lax.broadcasted_iota(jnp.int32, (spots, width), 0)
        == lax.broadcasted_iota(jnp.int32, (spots, width), 1) // TZ
    ).astype(F32)
    owners = jnp.dot(
        jnp.broadcast_to(owner, (8, spots)), expand, preferred_element_type=F32
    )[0:1]
    live = owners >= 0.0
    place_row = lax.broadcasted_iota(jnp.int32, (rows, width), 0)
    place_lane = lax.broadcasted_iota(jnp.int32, (rows, width), 1)
    spread_to = (
        ((place_row // TZ).astype(F32) == owners) & (place_row % TZ == place_lane % TZ)
    ).astype(F32)

    loads[0].wait()
    pl.semaphore_wait(barrier, n - 1)

    send_x_last(0)
    send_x_first(0, [S[0, 0, 0]])

    def send_tiles(k):
        target = lax.rem(me + 1 + k, n)
        there = pl.ds(pl.multiple_of(target * TZ, TZ), TZ)
        pltpu.make_async_remote_copy(
            packed.at[there], arrived.at[here], tile_send, tile_recv,
            device_id={"gx": target}, device_id_type=MESH,
        ).start()

    each(n - 1, send_tiles)
    send_y(0, [(S.at[0], 1)], [(S.at[0], 3), (S.at[0], 5)])

    for load in loads[1:]:
        load.wait()

    part = pl.ds(0, (n - 1) * TZ)
    pltpu.make_async_copy(arrived.at[part], arrived.at[part], tile_recv).wait()
    placed = lax.dot_general(
        arrived[...].T, spread_to, (((1,), (0,)), ((), ())), preferred_element_type=F32
    )
    for prop, field in enumerate((LAM, MU, BUO)):
        for i in range(nx):
            for ry in range(ny // TY):
                top = (prop * nx + i) * TY
                piece = placed[top:top + TY, ry * nz:(ry + 1) * nz]
                at = slice(ry * TY, (ry + 1) * TY)
                field[i, at, :] = jnp.where(
                    live[:, ry * nz:(ry + 1) * nz], piece, field[i, at, :]
                )

    y_of = lax.broadcasted_iota(jnp.int32, (ny, nz), 0)
    z_of = lax.broadcasted_iota(jnp.int32, (ny, nz), 1)

    def after_y(a, halo):
        return jnp.where(y_of == ny - 1, halo, pltpu.roll(a, ny - 1, 0))

    def before_y(a, halo):
        return jnp.where(y_of == 0, halo, pltpu.roll(a, 1, 0))

    def after_z(a):
        return jnp.where(z_of == nz - 1, 0.0, pltpu.roll(a, nz - 1, 1))

    def before_z(a):
        return jnp.where(z_of == 0, 0.0, pltpu.roll(a, 1, 1))

    order = [0, nx - 1] + list(range(1, nx - 1))
    for step in range(steps):
        last = step == steps - 1
        r = 2 * step
        s, v_old = S.at[step], V.at[step]
        v = last_v if last else V.at[step + 1]
        s_new = last_s if last else S.at[step + 1]
        m_new = last_m if last else M
        receive(r)

        def row_of(buf, r, comp, i):
            at = comp * nx + i
            return buf[r, at:at + 1, :]

        for i in order:
            scale = COURANT * BUO[i]
            xy, xz, yz = s[3, i], s[4, i], s[5, i]
            ahead = s[0, i + 1] if i < nx - 1 else xa_recv[r, 0].astype(F32)
            gx = (
                (ahead - s[0, i])
                + (xy - before_y(xy, row_of(yb_recv, r, 0, i)))
                + (xz - before_z(xz))
            )
            behind = s[3, i - 1] if i > 0 else xb_recv[r, 0]
            yy = s[1, i]
            gy = (
                (xy - behind)
                + (after_y(yy, row_of(ya_recv, r, 0, i)) - yy)
                + (yz - before_z(yz))
            )
            behind = s[4, i - 1] if i > 0 else xb_recv[r, 1]
            zz = s[2, i]
            gz = (
                (xz - behind)
                + (yz - before_y(yz, row_of(yb_recv, r, 1, i)))
                + (after_z(zz) - zz)
            )
            v[0, i] = v_old[0, i] + scale * gx
            v[1, i] = v_old[1, i] + scale * gy
            v[2, i] = v_old[2, i] + scale * gz
            if i == 0:
                send_x_first(r + 1, [v[1, 0], v[2, 0]])
            if i == nx - 1:
                send_x_last(r + 1)
        send_y(r + 1, [(v, 0), (v, 2)], [(v, 1)])

        r = r + 1
        receive(r)
        for i in order:
            lame, shear = LAM[i], MU[i]
            vx, vy, vz = v[0, i], v[1, i], v[2, i]
            behind = v[0, i - 1] if i > 0 else xb_recv[r, 0]
            ex = vx - behind
            ey = vy - before_y(vy, row_of(yb_recv, r, 0, i))
            ez = vz - before_z(vz)
            spread = lame * (ex + ey + ez)
            ahead_y = v[1, i + 1] if i < nx - 1 else xa_recv[r, 0].astype(F32)
            ahead_z = v[2, i + 1] if i < nx - 1 else xa_recv[r, 1].astype(F32)
            rates = (
                spread + 2.0 * shear * ex,
                spread + 2.0 * shear * ey,
                spread + 2.0 * shear * ez,
                shear * ((after_y(vx, row_of(ya_recv, r, 0, i)) - vx) + (ahead_y - vy)),
                shear * ((after_z(vx) - vx) + (ahead_z - vz)),
                shear * ((after_z(vy) - vy) + (after_y(vz, row_of(ya_recv, r, 1, i)) - vz)),
            )
            keep = DEC[i]
            drop = (1.0 - keep) * LOS[i]
            for c in range(6):
                m = keep * M[c, i] - drop * rates[c]
                m_new[c, i] = m
                new = s[c, i] + COURANT * (rates[c] + m)
                s_new[c, i] = new + source[step, i] if c < 3 else new
            if not last and i == 0:
                send_x_first(r + 1, [s_new[0, 0]])
            if not last and i == nx - 1:
                send_x_last(r + 1)
        if not last:
            send_y(r + 1, [(s_new, 1)], [(s_new, 3), (s_new, 5)])

    pltpu.make_async_copy(packed.at[part], packed.at[part], tile_send).wait()
    for r in range(2 * steps):
        copy_ya(r).wait_send()
        copy_yb(r).wait_send()
        pl.when(has_behind)(functools.partial(lambda q: copy_xa(q).wait_send(), r))
        pl.when(has_ahead)(functools.partial(lambda q: copy_xb(q).wait_send(), r))


def write(v, s, m, out_v, out_s, out_m, sems):
    stores = [
        pltpu.make_async_copy(src, dst.at[:, 0], sems.at[k])
        for k, (src, dst) in enumerate(((s, out_s), (m, out_m), (v, out_v)))
    ]
    for store in stores:
        store.start()
    for store in stores:
        store.wait()


def body(n, velocity, stress, memory, lame_lambda, lame_mu, buoyancy, decay, loss,
         tile_lambda, tile_mu, tile_buoy, tile_dest, brick_tiles, src_index, src_wave):
    steps = src_wave.shape[1]
    grid = lame_lambda.shape[1:]
    nx, ny, nz = grid
    rounds = 2 * steps
    hbm = pl.BlockSpec(memory_space=pltpu.HBM)
    vmem = pl.BlockSpec(memory_space=pltpu.VMEM)
    big = (velocity, stress, memory, lame_lambda, lame_mu, buoyancy, decay, loss)
    small = (tile_lambda, tile_mu, tile_buoy, tile_dest.reshape(1, -1), brick_tiles,
             src_index.reshape(1, -1), src_wave.T)
    states = pl.pallas_call(
        functools.partial(kernel, n, steps),
        out_shape=tuple(jax.ShapeDtypeStruct((c,) + grid, F32) for c in (3, 6, 6)),
        in_specs=[hbm] * (len(big) + len(small)),
        out_specs=(vmem,) * 3,
        scratch_shapes=[
            pltpu.VMEM((steps, 3) + grid, F32),
            pltpu.VMEM((steps, 6) + grid, F32),
            pltpu.VMEM((6,) + grid, F32),
        ] + [pltpu.VMEM(grid, F32)] * 5 + [pltpu.VMEM(a.shape, a.dtype) for a in small] + [
            pltpu.VMEM((n * TZ, 128), F32),
            pltpu.VMEM((n * TZ, 128), F32),
            pltpu.VMEM((steps,) + grid, F32),
            pltpu.VMEM((rounds, 2, ny, nz), jnp.bfloat16),
            pltpu.VMEM((rounds, 2, ny, nz), jnp.bfloat16),
            pltpu.VMEM((rounds, 2, ny, nz), F32),
            pltpu.VMEM((rounds, 8, nz), F32),
            pltpu.VMEM((rounds, 8, nz), F32),
            pltpu.VMEM((rounds, 8, nz), F32),
            pltpu.VMEM((rounds, 8, nz), F32),
            pltpu.SemaphoreType.DMA((8,)),
            pltpu.SemaphoreType.DMA((len(small),)),
            pltpu.SemaphoreType.DMA,
            pltpu.SemaphoreType.DMA,
            pltpu.SemaphoreType.DMA((4 * rounds,)),
            pltpu.SemaphoreType.DMA((4 * rounds,)),
        ],
        compiler_params=pltpu.CompilerParams(
            collective_id=0, has_side_effects=True, vmem_limit_bytes=VMEM_LIMIT
        ),
    )(*big, *small)
    return pl.pallas_call(
        write,
        out_shape=tuple(
            jax.ShapeDtypeStruct(a.shape, F32) for a in (velocity, stress, memory)
        ),
        in_specs=[vmem] * 3,
        out_specs=(hbm,) * 3,
        scratch_shapes=[pltpu.SemaphoreType.DMA((3,))],
    )(*states)


def solution(mesh):
    both = ("groups", "gx")
    field = P(None, both, None, None, None)
    single = P(both, None, None, None)
    return jax.shard_map(
        functools.partial(body, mesh.shape["gx"]),
        mesh=mesh,
        in_specs=(field,) * 3 + (single,) * 5 + (P(both, None),) * 3
        + (P(both), P(both, None), P(both), P(both, None)),
        out_specs=(field,) * 3,
        check_vma=False,
    )
```

```python
import functools

import jax
import jax.numpy as jnp
from jax import lax
from jax.experimental import pallas as pl
from jax.experimental.pallas import tpu as pltpu
from jax.sharding import PartitionSpec as P

MESH = pl.DeviceIdType.MESH
F32 = jnp.float32
PY = 8
TY = 8
TZ = 8
COURANT = 0.25
UNROLL = 16
VMEM_LIMIT = 64 * 1024 * 1024 - 1024 * 1024


def each(count, body):
    if count <= UNROLL:
        for k in range(count):
            body(k)
    else:
        lax.fori_loop(0, count, lambda k, c: (body(k), c)[1], 0)


def kernel(
    n, steps,
    vel, stress, mem, lam, mu, buo, dec, los,
    tile_l_in, tile_m_in, tile_b_in, dest_in, bricks_in, index_in, wave_in,
    last_v, last_s, last_m,
    V, S, M, LAM, MU, BUO, DEC, LOS,
    tile_l, tile_m, tile_b, dest, bricks, index, wave,
    packed, arrived, source,
    xa_send, xa_recv, xb_send, xb_recv, ya_send, ya_recv, yb_send, yb_recv,
    corner_send, corner_recv,
    load_sem, small_sem, tile_send, tile_recv, send_sem, recv_sem,
    corner_send_sem, corner_recv_sem,
):
    me = lax.axis_index("gx")
    nx, ny, nz = LAM.shape
    per_device = tile_l.shape[0]
    has_ahead = me + PY < n
    has_behind = me >= PY
    next_y = lax.rem(me + 1, n)
    prev_y = lax.rem(me + n - 1, n)

    barrier = pltpu.get_barrier_semaphore()

    def greet(k):
        pl.semaphore_signal(
            barrier, inc=1, device_id={"gx": lax.rem(me + 1 + k, n)}, device_id_type=MESH
        )

    each(n - 1, greet)

    small = [
        pltpu.make_async_copy(src, dst, small_sem.at[k])
        for k, (src, dst) in enumerate((
            (dest_in, dest), (tile_l_in, tile_l), (tile_m_in, tile_m), (tile_b_in, tile_b),
            (bricks_in, bricks), (index_in, index), (wave_in, wave),
        ))
    ]
    for load in small:
        load.start()
    loads = [
        pltpu.make_async_copy(stress.at[:, 0], S.at[0], load_sem.at[0]),
        pltpu.make_async_copy(buo.at[0], BUO, load_sem.at[1]),
        pltpu.make_async_copy(vel.at[:, 0], V.at[0], load_sem.at[2]),
        pltpu.make_async_copy(lam.at[0], LAM, load_sem.at[3]),
        pltpu.make_async_copy(mu.at[0], MU, load_sem.at[4]),
        pltpu.make_async_copy(dec.at[0], DEC, load_sem.at[5]),
        pltpu.make_async_copy(los.at[0], LOS, load_sem.at[6]),
        pltpu.make_async_copy(mem.at[:, 0], M, load_sem.at[7]),
    ]
    for load in loads:
        load.start()

    for load in small:
        load.wait()

    rows = n * TZ
    row = lax.broadcasted_iota(jnp.int32, (rows, per_device), 0)
    chosen = (dest[...] == row // TZ).astype(F32)
    cells = tile_l.shape[1]
    wide_row = lax.broadcasted_iota(jnp.int32, (rows, cells), 0)
    wide_lane = lax.broadcasted_iota(jnp.int32, (rows, cells), 1)
    same = wide_row % TZ == wide_lane % TZ
    fold_row = lax.broadcasted_iota(jnp.int32, (cells, 128), 0) // TZ
    fold_lane = lax.broadcasted_iota(jnp.int32, (cells, 128), 1)
    total = jnp.zeros((rows, 128), F32)
    for prop, tiles in enumerate((tile_l, tile_m, tile_b)):
        spread = jnp.dot(chosen, tiles[...].astype(F32), preferred_element_type=F32)
        spread = jnp.where(same, spread, 0.0)
        fold = (fold_lane == fold_row + prop * nx * TY).astype(F32)
        total = total + jnp.dot(spread, fold, preferred_element_type=F32)
    packed[...] = total
    ya_send[...] = jnp.zeros_like(ya_send)
    yb_send[...] = jnp.zeros_like(yb_send)
    here = pl.ds(pl.multiple_of(me * TZ, TZ), TZ)
    arrived[here, :] = packed[here, :]

    @pl.when(jnp.logical_not(has_ahead))
    def _():
        xa_recv[...] = jnp.zeros_like(xa_recv)

    @pl.when(jnp.logical_not(has_behind))
    def _():
        xb_recv[...] = jnp.zeros_like(xb_recv)

    def copy(r, k, send, recv, target):
        return pltpu.make_async_remote_copy(
            send, recv, send_sem.at[r * 4 + k], recv_sem.at[r * 4 + k],
            device_id={"gx": lax.rem(target + 2 * n, n)}, device_id_type=MESH,
        )

    def copy_xa(r):
        part = pl.ds(0, (1, 2, 1, 3)[min(r, 3)])
        return copy(r, 0, xa_send.at[r, part], xa_recv.at[r, part], me - PY)

    def copy_xb(r):
        part = pl.ds(0, (2, 1, 1, 3)[min(r, 3)])
        return copy(r, 1, xb_send.at[r, part], xb_recv.at[r, part], me + PY)

    def copy_ya(r):
        part = pl.ds(0, 8 if r < 3 else 16)
        return copy(r, 2, ya_send.at[r, part], ya_recv.at[r, part], me - 1)

    def copy_yb(r):
        part = pl.ds(0, 8 if r < 3 else 16)
        return copy(r, 3, yb_send.at[r, part], yb_recv.at[r, part], me + 1)

    def copy_corner(step, k):
        at = (step - 1) * 4 + k
        return pltpu.make_async_remote_copy(
            corner_send.at[at], corner_recv.at[at],
            corner_send_sem.at[at], corner_recv_sem.at[at],
            device_id={"gx": lax.rem(me + n + (PY + 1, -PY - 1, 1 - PY, PY - 1)[k], n)},
            device_id_type=MESH,
        )

    def send_x_first(r, planes):
        for c, plane in enumerate(planes):
            xa_send[r, c] = plane.astype(jnp.bfloat16)
        pl.when(has_behind)(lambda: copy_xa(r).start())

    def send_x_last(r, planes):
        for c, plane in enumerate(planes):
            xb_send[r, c] = plane
        pl.when(has_ahead)(lambda: copy_xb(r).start())

    def send_y(r, first, last):
        for c, part in enumerate(first):
            ya_send[r, c * nx:(c + 1) * nx, :] = part
        for c, part in enumerate(last):
            yb_send[r, c * nx:(c + 1) * nx, :] = part
        copy_ya(r).start()
        copy_yb(r).start()

    def receive(r):
        copy_ya(r).wait_recv()
        copy_yb(r).wait_recv()
        pl.when(has_ahead)(lambda: copy_xa(r).wait_recv())
        pl.when(has_behind)(lambda: copy_xb(r).wait_recv())

    elems = index.shape[1]
    cell = index[...]
    where_row = (cell // nz).astype(F32)
    where_lane = (cell % nz).astype(F32)
    eye = lax.broadcasted_iota(jnp.int32, (elems, elems), 0) == lax.broadcasted_iota(
        jnp.int32, (elems, elems), 1
    )
    lane_of = jnp.sum(jnp.where(eye, where_lane, 0.0), axis=1, keepdims=True)
    on_row = (
        lax.broadcasted_iota(jnp.int32, (nx * ny, elems), 0).astype(F32) == where_row
    ).astype(F32)
    on_lane = (
        lax.broadcasted_iota(jnp.int32, (elems, nz), 1).astype(F32) == lane_of
    ).astype(F32)
    for step in range(steps):
        amounts = on_row * wave[step:step + 1, :]
        source[step] = jnp.dot(
            amounts, on_lane, preferred_element_type=F32, precision=lax.Precision.HIGHEST
        ).reshape(nx, ny, nz)

    spots = bricks.shape[1]
    width = spots * TZ
    owner = jnp.floor((bricks[...].astype(F32) + 0.5) * (1.0 / per_device))
    expand = (
        lax.broadcasted_iota(jnp.int32, (spots, width), 0)
        == lax.broadcasted_iota(jnp.int32, (spots, width), 1) // TZ
    ).astype(F32)
    owners = jnp.dot(
        jnp.broadcast_to(owner, (8, spots)), expand, preferred_element_type=F32
    )[0:1]
    live = owners >= 0.0
    place_row = lax.broadcasted_iota(jnp.int32, (rows, width), 0)
    place_lane = lax.broadcasted_iota(jnp.int32, (rows, width), 1)
    spread_to = (
        ((place_row // TZ).astype(F32) == owners) & (place_row % TZ == place_lane % TZ)
    ).astype(F32)

    loads[0].wait()
    pl.semaphore_wait(barrier, n - 1)

    send_x_last(0, [S[0, 3, nx - 1], S[0, 4, nx - 1]])
    send_x_first(0, [S[0, 0, 0]])

    def send_tiles(k):
        target = lax.rem(me + 1 + k, n)
        there = pl.ds(pl.multiple_of(target * TZ, TZ), TZ)
        pltpu.make_async_remote_copy(
            packed.at[there], arrived.at[here], tile_send, tile_recv,
            device_id={"gx": target}, device_id_type=MESH,
        ).start()

    each(n - 1, send_tiles)
    send_y(0, [S[0, 1, :, 0, :]], [S[0, 3, :, ny - 1, :], S[0, 5, :, ny - 1, :]])

    for load in loads[1:]:
        load.wait()

    part = pl.ds(0, (n - 1) * TZ)
    pltpu.make_async_copy(arrived.at[part], arrived.at[part], tile_recv).wait()
    placed = lax.dot_general(
        arrived[...].T, spread_to, (((1,), (0,)), ((), ())), preferred_element_type=F32
    )
    for prop, field in enumerate((LAM, MU, BUO)):
        for i in range(nx):
            for ry in range(ny // TY):
                top = (prop * nx + i) * TY
                piece = placed[top:top + TY, ry * nz:(ry + 1) * nz]
                at = slice(ry * TY, (ry + 1) * TY)
                field[i, at, :] = jnp.where(
                    live[:, ry * nz:(ry + 1) * nz], piece, field[i, at, :]
                )

    def after_y(a, halo):
        y_of = lax.broadcasted_iota(jnp.int32, a.shape, 0)
        return jnp.where(y_of == ny - 1, halo, pltpu.roll(a, ny - 1, 0))

    def before_y(a, halo):
        y_of = lax.broadcasted_iota(jnp.int32, a.shape, 0)
        return jnp.where(y_of == 0, halo, pltpu.roll(a, 1, 0))

    def after_z(a):
        z_of = lax.broadcasted_iota(jnp.int32, a.shape, 1)
        return jnp.where(z_of == nz - 1, 0.0, pltpu.roll(a, nz - 1, 1))

    def before_z(a):
        z_of = lax.broadcasted_iota(jnp.int32, a.shape, 1)
        return jnp.where(z_of == 0, 0.0, pltpu.roll(a, 1, 1))

    def only_y(plane_row, y):
        at = lax.broadcasted_iota(jnp.int32, (ny, nz), 0) == y
        return jnp.where(at, plane_row, 0.0)

    def only_x(one_row, x, allowed):
        at = lax.broadcasted_iota(jnp.int32, (nx, nz), 0) == x
        return jnp.where(at & allowed, one_row, 0.0)

    zero_row = jnp.zeros((1, nz), F32)

    def after_x(a):
        return jnp.concatenate([a[1:], zero_row], axis=0)

    def before_x(a):
        return jnp.concatenate([zero_row, a[:-1]], axis=0)

    def send_first_partial(r, s, v):
        scale = COURANT * BUO[0]
        xy, yy, xz, yz, zz = s[3, 0], s[1, 0], s[4, 0], s[5, 0], s[2, 0]
        gy = xy + (after_y(yy, 0.0) - yy) + (yz - before_z(yz))
        gz = xz + (yz - before_y(yz, 0.0)) + (after_z(zz) - zz)
        send_x_first(r, [s[0, 0], v[1, 0] + scale * gy, v[2, 0] + scale * gz])

    def send_last_partial(r, s, v):
        e = nx - 1
        xx, xy, xz = s[0, e], s[3, e], s[4, e]
        gx = (xy - before_y(xy, 0.0)) - xx + (xz - before_z(xz))
        send_x_last(r, [xy, xz, v[0, e] + COURANT * BUO[e] * gx])

    def send_corners(step, s):
        e = nx - 1
        at = (step - 1) * 4
        corner_send[at] = jnp.broadcast_to(s[3, e, ny - 1:, :], (8, nz))
        corner_send[at + 1, 0:4, :] = jnp.broadcast_to(s[1, 0, 0:1, :], (4, nz))
        corner_send[at + 1, 4:8, :] = jnp.broadcast_to(s[0, 0, 0:1, :], (4, nz))
        corner_send[at + 2] = jnp.broadcast_to(s[5, 0, ny - 1:, :], (8, nz))
        corner_send[at + 3] = jnp.broadcast_to(s[4, e, 0:1, :], (8, nz))
        for k in range(4):
            copy_corner(step, k).start()

    def send_y_partial(r, s, v):
        xx, yy, zz, xy, xz, yz = (s[c, :, 0, :] for c in range(6))
        scale = COURANT * BUO[:, 0, :]
        gx = (after_x(xx) - xx) + xy + (xz - before_z(xz))
        gz = (xz - before_x(xz)) + yz + (after_z(zz) - zz)
        first = [yy, v[0, :, 0, :] + scale * gx, v[2, :, 0, :] + scale * gz]
        yy, xy, yz = (s[c, :, ny - 1, :] for c in (1, 3, 5))
        gy = (xy - before_x(xy)) - yy + (yz - before_z(yz))
        scale = COURANT * BUO[:, ny - 1, :]
        send_y(r, first, [xy, yz, v[1, :, ny - 1, :] + scale * gy])

    order = [0, nx - 1] + list(range(1, nx - 1))
    for step in range(steps):
        last = step == steps - 1
        r = 0 if step == 0 else step + 2
        s, v_old = S.at[step], V.at[step]
        v = last_v if last else V.at[step + 1]
        s_new = last_s if last else S.at[step + 1]
        m_new = last_m if last else M
        receive(r)

        def row_of(buf, r, comp, i):
            at = comp * nx + i
            return buf[r, at:at + 1, :]

        for i in order:
            scale = COURANT * BUO[i]
            xy, xz, yz = s[3, i], s[4, i], s[5, i]
            ahead = s[0, i + 1] if i < nx - 1 else xa_recv[r, 0].astype(F32)
            gx = (
                (ahead - s[0, i])
                + (xy - before_y(xy, row_of(yb_recv, r, 0, i)))
                + (xz - before_z(xz))
            )
            behind = s[3, i - 1] if i > 0 else xb_recv[r, 0]
            yy = s[1, i]
            gy = (
                (xy - behind)
                + (after_y(yy, row_of(ya_recv, r, 0, i)) - yy)
                + (yz - before_z(yz))
            )
            behind = s[4, i - 1] if i > 0 else xb_recv[r, 1]
            zz = s[2, i]
            gz = (
                (xz - behind)
                + (yz - before_y(yz, row_of(yb_recv, r, 1, i)))
                + (after_z(zz) - zz)
            )
            v[0, i] = v_old[0, i] + scale * gx
            v[1, i] = v_old[1, i] + scale * gy
            v[2, i] = v_old[2, i] + scale * gz
            if step == 0 and i == 0:
                send_x_first(1, [v[1, 0], v[2, 0]])
            if step == 0 and i == nx - 1:
                send_x_last(1, [v[0, i]])
        if step == 0:
            send_y(1, [v[0, :, 0, :], v[2, :, 0, :]], [v[1, :, ny - 1, :]])
            if not last:
                send_x_first(2, [BUO[0]])
                send_x_last(2, [BUO[nx - 1]])
                send_y(2, [BUO[:, 0, :]], [BUO[:, ny - 1, :]])
            receive(1)
            v_behind_x = xb_recv[1, 0]
            v_ahead_y, v_ahead_z = xa_recv[1, 0].astype(F32), xa_recv[1, 1].astype(F32)
            v_after_x, v_after_z = ya_recv[1, 0:nx, :], ya_recv[1, nx:2 * nx, :]
            v_before_y = yb_recv[1, 0:nx, :]
        else:
            if step == 1:
                receive(2)
            at = (step - 1) * 4
            for k in range(4):
                copy_corner(step, k).wait_recv()
            c_xy = corner_recv[at, 0:1, :]
            c_yy, c_xx = corner_recv[at + 1, 0:1, :], corner_recv[at + 1, 4:5, :]
            c_yz = corner_recv[at + 2, 0:1, :]
            c_xz = corner_recv[at + 3, 0:1, :]
            e = nx - 1
            scale = COURANT * xb_recv[2, 0]
            v_behind_x = xb_recv[r, 2] + scale * (s[0, 0] - only_y(c_xy, 0))
            scale = COURANT * xa_recv[2, 0].astype(F32)
            v_ahead_y = xa_recv[r, 1].astype(F32) + scale * (only_y(c_yy, ny - 1) - s[3, e])
            v_ahead_z = xa_recv[r, 2].astype(F32) - scale * (only_y(c_yz, 0) + s[4, e])
            scale = COURANT * ya_recv[2, 0:nx, :]
            v_after_x = ya_recv[r, nx:2 * nx, :] + scale * (
                only_x(c_xx, e, next_y + PY < n) - s[3, :, ny - 1, :]
            )
            v_after_z = ya_recv[r, 2 * nx:3 * nx, :] - scale * (
                only_x(c_xz, 0, next_y >= PY) + s[5, :, ny - 1, :]
            )
            scale = COURANT * yb_recv[2, 0:nx, :]
            v_before_y = yb_recv[r, 2 * nx:3 * nx, :] + scale * (
                s[1, :, 0, :] - only_x(c_xy, 0, prev_y >= PY)
            )

        for i in order:
            lame, shear = LAM[i], MU[i]
            vx, vy, vz = v[0, i], v[1, i], v[2, i]
            behind = v[0, i - 1] if i > 0 else v_behind_x
            ex = vx - behind
            ey = vy - before_y(vy, v_before_y[i:i + 1])
            ez = vz - before_z(vz)
            spread = lame * (ex + ey + ez)
            ahead_y = v[1, i + 1] if i < nx - 1 else v_ahead_y
            ahead_z = v[2, i + 1] if i < nx - 1 else v_ahead_z
            rates = (
                spread + 2.0 * shear * ex,
                spread + 2.0 * shear * ey,
                spread + 2.0 * shear * ez,
                shear * ((after_y(vx, v_after_x[i:i + 1]) - vx) + (ahead_y - vy)),
                shear * ((after_z(vx) - vx) + (ahead_z - vz)),
                shear * ((after_z(vy) - vy) + (after_y(vz, v_after_z[i:i + 1]) - vz)),
            )
            keep = DEC[i]
            drop = (1.0 - keep) * LOS[i]
            for c in range(6):
                m = keep * M[c, i] - drop * rates[c]
                m_new[c, i] = m
                new = s[c, i] + COURANT * (rates[c] + m)
                s_new[c, i] = new + source[step, i] if c < 3 else new
            if not last and i == 0:
                send_first_partial(step + 3, s_new, v)
            if not last and i == nx - 1:
                send_last_partial(step + 3, s_new, v)
        if not last:
            send_y_partial(step + 3, s_new, v)
            send_corners(step + 1, s_new)

    pltpu.make_async_copy(packed.at[part], packed.at[part], tile_send).wait()
    for r in range(2 + steps if steps > 1 else 2):
        copy_ya(r).wait_send()
        copy_yb(r).wait_send()
        pl.when(has_behind)(functools.partial(lambda q: copy_xa(q).wait_send(), r))
        pl.when(has_ahead)(functools.partial(lambda q: copy_xb(q).wait_send(), r))
    for step in range(1, steps):
        for k in range(4):
            copy_corner(step, k).wait_send()


def write(v, s, m, out_v, out_s, out_m, sems):
    stores = [
        pltpu.make_async_copy(src, dst.at[:, 0], sems.at[k])
        for k, (src, dst) in enumerate(((s, out_s), (m, out_m), (v, out_v)))
    ]
    for store in stores:
        store.start()
    for store in stores:
        store.wait()


def body(n, velocity, stress, memory, lame_lambda, lame_mu, buoyancy, decay, loss,
         tile_lambda, tile_mu, tile_buoy, tile_dest, brick_tiles, src_index, src_wave):
    steps = src_wave.shape[1]
    grid = lame_lambda.shape[1:]
    nx, ny, nz = grid
    rounds = 2 + steps
    corners = 4 * max(steps - 1, 1)
    hbm = pl.BlockSpec(memory_space=pltpu.HBM)
    vmem = pl.BlockSpec(memory_space=pltpu.VMEM)
    big = (velocity, stress, memory, lame_lambda, lame_mu, buoyancy, decay, loss)
    small = (tile_lambda, tile_mu, tile_buoy, tile_dest.reshape(1, -1), brick_tiles,
             src_index.reshape(1, -1), src_wave.T)
    states = pl.pallas_call(
        functools.partial(kernel, n, steps),
        out_shape=tuple(jax.ShapeDtypeStruct((c,) + grid, F32) for c in (3, 6, 6)),
        in_specs=[hbm] * (len(big) + len(small)),
        out_specs=(vmem,) * 3,
        scratch_shapes=[
            pltpu.VMEM((steps, 3) + grid, F32),
            pltpu.VMEM((steps, 6) + grid, F32),
            pltpu.VMEM((6,) + grid, F32),
        ] + [pltpu.VMEM(grid, F32)] * 5 + [pltpu.VMEM(a.shape, a.dtype) for a in small] + [
            pltpu.VMEM((n * TZ, 128), F32),
            pltpu.VMEM((n * TZ, 128), F32),
            pltpu.VMEM((steps,) + grid, F32),
            pltpu.VMEM((rounds, 3, ny, nz), jnp.bfloat16),
            pltpu.VMEM((rounds, 3, ny, nz), jnp.bfloat16),
            pltpu.VMEM((rounds, 3, ny, nz), F32),
            pltpu.VMEM((rounds, 3, ny, nz), F32),
        ] + [pltpu.VMEM((rounds, 16, nz), F32)] * 4
        + [pltpu.VMEM((corners, 8, nz), F32)] * 2 + [
            pltpu.SemaphoreType.DMA((8,)),
            pltpu.SemaphoreType.DMA((len(small),)),
            pltpu.SemaphoreType.DMA,
            pltpu.SemaphoreType.DMA,
            pltpu.SemaphoreType.DMA((4 * rounds,)),
            pltpu.SemaphoreType.DMA((4 * rounds,)),
            pltpu.SemaphoreType.DMA((corners,)),
            pltpu.SemaphoreType.DMA((corners,)),
        ],
        compiler_params=pltpu.CompilerParams(
            collective_id=0, has_side_effects=True, vmem_limit_bytes=VMEM_LIMIT
        ),
    )(*big, *small)
    return pl.pallas_call(
        write,
        out_shape=tuple(
            jax.ShapeDtypeStruct(a.shape, F32) for a in (velocity, stress, memory)
        ),
        in_specs=[vmem] * 3,
        out_specs=(hbm,) * 3,
        scratch_shapes=[pltpu.SemaphoreType.DMA((3,))],
    )(*states)


def solution(mesh):
    both = ("groups", "gx")
    field = P(None, both, None, None, None)
    single = P(both, None, None, None)
    return jax.shard_map(
        functools.partial(body, mesh.shape["gx"]),
        mesh=mesh,
        in_specs=(field,) * 3 + (single,) * 5 + (P(both, None),) * 3
        + (P(both), P(both, None), P(both), P(both, None)),
        out_specs=(field,) * 3,
        check_vma=False,
    )
```

```python
import functools

import jax
import jax.numpy as jnp
from jax import lax
from jax.experimental import pallas as pl
from jax.experimental.pallas import tpu as pltpu
from jax.sharding import PartitionSpec as P

MESH = pl.DeviceIdType.MESH
F32 = jnp.float32
PY = 8
TY = 8
TZ = 8
COURANT = 0.25
UNROLL = 16
VMEM_LIMIT = 64 * 1024 * 1024 - 1024 * 1024


def each(count, body):
    if count <= UNROLL:
        for k in range(count):
            body(k)
    else:
        lax.fori_loop(0, count, lambda k, c: (body(k), c)[1], 0)


def kernel(
    n, steps,
    vel, stress, mem, lam, mu, buo, dec, los,
    tile_l_in, tile_m_in, tile_b_in, dest_in, bricks_in, index_in, wave_in,
    last_v, last_s, last_m,
    V, S, M, LAM, MU, BUO, DEC, LOS,
    tile_l, tile_m, tile_b, dest, bricks, index, wave,
    packed, arrived, source,
    xa_send, xa_recv, xb_send, xb_recv, ya_send, ya_recv, yb_send, yb_recv,
    corner_send, corner_recv, table_send, table_recv,
    load_sem, small_sem, tile_send, tile_recv, send_sem, recv_sem,
    corner_send_sem, corner_recv_sem,
):
    me = lax.axis_index("gx")
    nx, ny, nz = LAM.shape
    per_device = tile_l.shape[0]
    has_ahead = me + PY < n
    has_behind = me >= PY
    next_y = lax.rem(me + 1, n)
    prev_y = lax.rem(me + n - 1, n)

    barrier = pltpu.get_barrier_semaphore()

    def greet(k):
        pl.semaphore_signal(
            barrier, inc=1, device_id={"gx": lax.rem(me + 1 + k, n)}, device_id_type=MESH
        )

    each(n - 1, greet)

    small = [
        pltpu.make_async_copy(src, dst, small_sem.at[k])
        for k, (src, dst) in enumerate((
            (dest_in, dest), (tile_l_in, tile_l), (tile_m_in, tile_m), (tile_b_in, tile_b),
            (bricks_in, bricks), (index_in, index), (wave_in, wave),
        ))
    ]
    for load in small:
        load.start()
    loads = [
        pltpu.make_async_copy(stress.at[:, 0], S.at[0], load_sem.at[0]),
        pltpu.make_async_copy(buo.at[0], BUO, load_sem.at[1]),
        pltpu.make_async_copy(vel.at[:, 0], V.at[0], load_sem.at[2]),
        pltpu.make_async_copy(lam.at[0], LAM, load_sem.at[3]),
        pltpu.make_async_copy(mu.at[0], MU, load_sem.at[4]),
        pltpu.make_async_copy(dec.at[0], DEC, load_sem.at[5]),
        pltpu.make_async_copy(los.at[0], LOS, load_sem.at[6]),
        pltpu.make_async_copy(mem.at[:, 0], M, load_sem.at[7]),
    ]
    for load in loads:
        load.start()

    for load in small:
        load.wait()

    rows = n * TZ
    row = lax.broadcasted_iota(jnp.int32, (rows, per_device), 0)
    chosen = (dest[...] == row // TZ).astype(F32)
    cells = tile_l.shape[1]
    wide_row = lax.broadcasted_iota(jnp.int32, (rows, cells), 0)
    wide_lane = lax.broadcasted_iota(jnp.int32, (rows, cells), 1)
    same = wide_row % TZ == wide_lane % TZ
    fold_row = lax.broadcasted_iota(jnp.int32, (cells, 128), 0) // TZ
    fold_lane = lax.broadcasted_iota(jnp.int32, (cells, 128), 1)
    total = jnp.zeros((rows, 128), F32)
    for prop, tiles in enumerate((tile_l, tile_m, tile_b)):
        spread = jnp.dot(chosen, tiles[...].astype(F32), preferred_element_type=F32)
        spread = jnp.where(same, spread, 0.0)
        fold = (fold_lane == fold_row + prop * nx * TY).astype(F32)
        total = total + jnp.dot(spread, fold, preferred_element_type=F32)
    there = row // TZ
    is_tile = dest[...] >= 0
    lanes = 3 * nx * TY
    tile_row = lax.broadcasted_iota(jnp.int32, (cells, 128), 0) // TZ
    for meant, fold in (
        ((dest[...] + PY == there) & is_tile,
         (tile_row - (nx - 1) * TY == fold_lane - lanes) & (tile_row >= (nx - 1) * TY)),
        (dest[...] - PY == there,
         (tile_row == fold_lane - (lanes + TY)) & (tile_row < TY)),
        ((jnp.where(dest[...] == n - 1, 0, dest[...] + 1) == there) & is_tile,
         (tile_row % TY == TY - 1) & (tile_row // TY == fold_lane - (lanes + 2 * TY))),
        ((jnp.where(dest[...] == 0, n - 1, dest[...] - 1) == there) & is_tile,
         (tile_row % TY == 0) & (tile_row // TY == fold_lane - (lanes + 2 * TY + nx))),
    ):
        spread = jnp.dot(meant.astype(F32), tile_b[...].astype(F32), preferred_element_type=F32)
        spread = jnp.where(same, spread, 0.0)
        total = total + jnp.dot(spread, fold.astype(F32), preferred_element_type=F32)
    packed[...] = total
    ya_send[...] = jnp.zeros_like(ya_send)
    yb_send[...] = jnp.zeros_like(yb_send)
    here = pl.ds(pl.multiple_of(me * TZ, TZ), TZ)
    arrived[here, :] = packed[here, :]

    @pl.when(jnp.logical_not(has_ahead))
    def _():
        xa_recv[...] = jnp.zeros_like(xa_recv)
        table_recv[0] = jnp.full(table_recv.shape[1:], -1.0, F32)

    @pl.when(jnp.logical_not(has_behind))
    def _():
        xb_recv[...] = jnp.zeros_like(xb_recv)
        table_recv[1] = jnp.full(table_recv.shape[1:], -1.0, F32)

    def copy(k, send, recv, target):
        return pltpu.make_async_remote_copy(
            send, recv, send_sem.at[k], recv_sem.at[k],
            device_id={"gx": lax.rem(target + 2 * n, n)}, device_id_type=MESH,
        )

    def copy_xa(r):
        part = pl.ds(0, 6 if r == 0 else 3)
        return copy(r * 4, xa_send.at[r, part], xa_recv.at[r, part], me - PY)

    def copy_xb(r):
        part = pl.ds(0, 5 if r == 0 else 3)
        return copy(r * 4 + 1, xb_send.at[r, part], xb_recv.at[r, part], me + PY)

    def copy_ya(r):
        part = pl.ds(0, 32 if r == 0 else 16)
        return copy(r * 4 + 2, ya_send.at[r, part], ya_recv.at[r, part], me - 1)

    def copy_yb(r):
        part = pl.ds(0, 32 if r == 0 else 16)
        return copy(r * 4 + 3, yb_send.at[r, part], yb_recv.at[r, part], me + 1)

    def copy_table_a():
        return copy(4 * steps, table_send, table_recv.at[0], me - PY)

    def copy_table_b():
        return copy(4 * steps + 1, table_send, table_recv.at[1], me + PY)

    def copy_corner(step, k):
        at = step * 4 + k
        return pltpu.make_async_remote_copy(
            corner_send.at[at], corner_recv.at[at],
            corner_send_sem.at[at], corner_recv_sem.at[at],
            device_id={"gx": lax.rem(me + n + (PY + 1, -PY - 1, 1 - PY, PY - 1)[k], n)},
            device_id_type=MESH,
        )

    def send_x_first(r, planes):
        for c, plane in enumerate(planes):
            xa_send[r, c] = plane.astype(jnp.bfloat16)
        pl.when(has_behind)(lambda: copy_xa(r).start())

    def send_x_last(r, planes):
        for c, plane in enumerate(planes):
            xb_send[r, c] = plane
        pl.when(has_ahead)(lambda: copy_xb(r).start())

    def send_y(r, first, last):
        for c, part in enumerate(first):
            ya_send[r, c * nx:c * nx + part.shape[0], :] = part
        for c, part in enumerate(last):
            yb_send[r, c * nx:c * nx + part.shape[0], :] = part
        copy_ya(r).start()
        copy_yb(r).start()

    def receive(r):
        copy_ya(r).wait_recv()
        copy_yb(r).wait_recv()
        pl.when(has_ahead)(lambda: copy_xa(r).wait_recv())
        pl.when(has_behind)(lambda: copy_xb(r).wait_recv())

    def after_y(a, halo):
        y_of = lax.broadcasted_iota(jnp.int32, a.shape, 0)
        return jnp.where(y_of == ny - 1, halo, pltpu.roll(a, ny - 1, 0))

    def before_y(a, halo):
        y_of = lax.broadcasted_iota(jnp.int32, a.shape, 0)
        return jnp.where(y_of == 0, halo, pltpu.roll(a, 1, 0))

    def after_z(a):
        z_of = lax.broadcasted_iota(jnp.int32, a.shape, 1)
        return jnp.where(z_of == nz - 1, 0.0, pltpu.roll(a, nz - 1, 1))

    def before_z(a):
        z_of = lax.broadcasted_iota(jnp.int32, a.shape, 1)
        return jnp.where(z_of == 0, 0.0, pltpu.roll(a, 1, 1))

    def only_y(plane_row, y):
        at = lax.broadcasted_iota(jnp.int32, (ny, nz), 0) == y
        return jnp.where(at, plane_row, 0.0)

    def only_x(one_row, x, allowed):
        at = lax.broadcasted_iota(jnp.int32, (nx, nz), 0) == x
        return jnp.where(at & allowed, one_row, 0.0)

    zero_row = jnp.zeros((1, nz), F32)

    def after_x(a):
        return jnp.concatenate([a[1:], zero_row], axis=0)

    def before_x(a):
        return jnp.concatenate([zero_row, a[:-1]], axis=0)

    def send_first_partial(r, s, v):
        scale = COURANT * BUO[0]
        xy, yy, xz, yz, zz = s[3, 0], s[1, 0], s[4, 0], s[5, 0], s[2, 0]
        gy = xy + (after_y(yy, 0.0) - yy) + (yz - before_z(yz))
        gz = xz + (yz - before_y(yz, 0.0)) + (after_z(zz) - zz)
        if r == 0:
            send_x_first(r, [s[0, 0], v[1, 0], v[2, 0], gy, gz, BUO[0]])
        else:
            send_x_first(r, [s[0, 0], v[1, 0] + scale * gy, v[2, 0] + scale * gz])

    def send_last_partial(r, s, v):
        e = nx - 1
        xx, xy, xz = s[0, e], s[3, e], s[4, e]
        gx = (xy - before_y(xy, 0.0)) - xx + (xz - before_z(xz))
        if r == 0:
            send_x_last(r, [xy, xz, v[0, e], gx, BUO[e]])
        else:
            send_x_last(r, [xy, xz, v[0, e] + COURANT * BUO[e] * gx])

    def send_corners(step, s):
        e = nx - 1
        at = step * 4
        corner_send[at] = jnp.broadcast_to(s[3, e, ny - 1:, :], (8, nz))
        corner_send[at + 1, 0:4, :] = jnp.broadcast_to(s[1, 0, 0:1, :], (4, nz))
        corner_send[at + 1, 4:8, :] = jnp.broadcast_to(s[0, 0, 0:1, :], (4, nz))
        corner_send[at + 2] = jnp.broadcast_to(s[5, 0, ny - 1:, :], (8, nz))
        corner_send[at + 3] = jnp.broadcast_to(s[4, e, 0:1, :], (8, nz))
        for k in range(4):
            copy_corner(step, k).start()

    def send_y_partial(r, s, v):
        xx, yy, zz, xy, xz, yz = (s[c, :, 0, :] for c in range(6))
        scale = COURANT * BUO[:, 0, :]
        gx = (after_x(xx) - xx) + xy + (xz - before_z(xz))
        gz = (xz - before_x(xz)) + yz + (after_z(zz) - zz)
        buoy = BUO[:, 0, :]
        vx, vz = v[0, :, 0, :], v[2, :, 0, :]
        if r == 0:
            first = [yy, vx, vz, gx, gz, buoy, table_send[0:1, :]]
        else:
            first = [yy, vx + scale * gx, vz + scale * gz]
        yy, xy, yz = (s[c, :, ny - 1, :] for c in (1, 3, 5))
        gy = (xy - before_x(xy)) - yy + (yz - before_z(yz))
        buoy = BUO[:, ny - 1, :]
        vy = v[1, :, ny - 1, :]
        if r == 0:
            bands = ny // TY
            last = [xy, yz, vy, gy, buoy, table_send[bands - 1:bands, :]]
        else:
            last = [xy, yz, vy + COURANT * buoy * gy]
        send_y(r, first, last)

    elems = index.shape[1]
    cell = index[...]
    where_row = (cell // nz).astype(F32)
    where_lane = (cell % nz).astype(F32)
    eye = lax.broadcasted_iota(jnp.int32, (elems, elems), 0) == lax.broadcasted_iota(
        jnp.int32, (elems, elems), 1
    )
    lane_of = jnp.sum(jnp.where(eye, where_lane, 0.0), axis=1, keepdims=True)
    on_row = (
        lax.broadcasted_iota(jnp.int32, (nx * ny, elems), 0).astype(F32) == where_row
    ).astype(F32)
    on_lane = (
        lax.broadcasted_iota(jnp.int32, (elems, nz), 1).astype(F32) == lane_of
    ).astype(F32)
    for step in range(steps):
        amounts = on_row * wave[step:step + 1, :]
        source[step] = jnp.dot(
            amounts, on_lane, preferred_element_type=F32, precision=lax.Precision.HIGHEST
        ).reshape(nx, ny, nz)

    spots = bricks.shape[1]
    width = spots * TZ
    owner = jnp.floor((bricks[...].astype(F32) + 0.5) * (1.0 / per_device))
    expand = (
        lax.broadcasted_iota(jnp.int32, (spots, width), 0)
        == lax.broadcasted_iota(jnp.int32, (spots, width), 1) // TZ
    ).astype(F32)
    owners = jnp.dot(
        jnp.broadcast_to(owner, (8, spots)), expand, preferred_element_type=F32
    )[0:1]
    live = owners >= 0.0
    place_row = lax.broadcasted_iota(jnp.int32, (rows, width), 0)
    place_lane = lax.broadcasted_iota(jnp.int32, (rows, width), 1)
    spread_to = (
        ((place_row // TZ).astype(F32) == owners) & (place_row % TZ == place_lane % TZ)
    ).astype(F32)

    table_send[...] = jnp.zeros_like(table_send)
    for ry in range(ny // TY):
        table_send[ry:ry + 1, :] = owners[:, ry * nz:(ry + 1) * nz]
    for load in loads[:3]:
        load.wait()
    pl.semaphore_wait(barrier, n - 1)

    send_last_partial(0, S.at[0], V.at[0])
    send_first_partial(0, S.at[0], V.at[0])
    pl.when(has_behind)(lambda: copy_table_a().start())
    pl.when(has_ahead)(lambda: copy_table_b().start())

    def send_tiles(k):
        target = lax.rem(me + 1 + k, n)
        there = pl.ds(pl.multiple_of(target * TZ, TZ), TZ)
        pltpu.make_async_remote_copy(
            packed.at[there], arrived.at[here], tile_send, tile_recv,
            device_id={"gx": target}, device_id_type=MESH,
        ).start()

    each(n - 1, send_tiles)
    send_y_partial(0, S.at[0], V.at[0])
    send_corners(0, S.at[0])

    for load in loads[3:]:
        load.wait()

    part = pl.ds(0, (n - 1) * TZ)
    pltpu.make_async_copy(arrived.at[part], arrived.at[part], tile_recv).wait()
    got = arrived[...].T
    placed = lax.dot_general(
        got, spread_to, (((1,), (0,)), ((), ())), preferred_element_type=F32
    )
    for prop, field in enumerate((LAM, MU, BUO)):
        for i in range(nx):
            for ry in range(ny // TY):
                top = (prop * nx + i) * TY
                piece = placed[top:top + TY, ry * nz:(ry + 1) * nz]
                at = slice(ry * TY, (ry + 1) * TY)
                field[i, at, :] = jnp.where(
                    live[:, ry * nz:(ry + 1) * nz], piece, field[i, at, :]
                )

    near_row = lax.broadcasted_iota(jnp.int32, (rows, nz), 0)
    near_lane = lax.broadcasted_iota(jnp.int32, (rows, nz), 1)
    near_same = near_row % TZ == near_lane % TZ
    near_brick = (near_row // TZ).astype(F32)

    def near(top, table, background):
        where_to = ((near_brick == table) & near_same).astype(F32)
        piece = jnp.dot(got[top:top + 8], where_to, preferred_element_type=F32)
        return jnp.where(table >= 0.0, piece, background)

    receive(0)
    pl.when(has_ahead)(lambda: copy_table_a().wait_recv())
    pl.when(has_behind)(lambda: copy_table_b().wait_recv())
    behind_parts, ahead_parts = [], []
    for ry in range(ny // TY):
        at = slice(ry * TY, (ry + 1) * TY)
        behind_parts.append(near(lanes, table_recv[1, ry:ry + 1, :], xb_recv[0, 4, at, :]))
        ahead_parts.append(
            near(lanes + TY, table_recv[0, ry:ry + 1, :], xa_recv[0, 5].astype(F32)[at])
        )
    scale_behind = COURANT * jnp.concatenate(behind_parts, axis=0)
    scale_ahead = COURANT * jnp.concatenate(ahead_parts, axis=0)
    both = jnp.concatenate(
        [yb_recv[0, 4 * nx:5 * nx, :], ya_recv[0, 5 * nx:6 * nx, :]], axis=0
    )
    scale_before = COURANT * near(lanes + 2 * TY, yb_recv[0, 5 * nx:5 * nx + 1, :], both)[0:nx]
    scale_after = COURANT * near(
        lanes + 2 * TY, ya_recv[0, 6 * nx:6 * nx + 1, :], both
    )[nx:2 * nx]

    order = [0, nx - 1] + list(range(1, nx - 1))
    for step in range(steps):
        last = step == steps - 1
        r = step
        s, v_old = S.at[step], V.at[step]
        v = last_v if last else V.at[step + 1]
        s_new = last_s if last else S.at[step + 1]
        m_new = last_m if last else M
        if step > 0:
            receive(r)

        def row_of(buf, r, comp, i):
            at = comp * nx + i
            return buf[r, at:at + 1, :]

        for i in order:
            scale = COURANT * BUO[i]
            xy, xz, yz = s[3, i], s[4, i], s[5, i]
            ahead = s[0, i + 1] if i < nx - 1 else xa_recv[r, 0].astype(F32)
            gx = (
                (ahead - s[0, i])
                + (xy - before_y(xy, row_of(yb_recv, r, 0, i)))
                + (xz - before_z(xz))
            )
            behind = s[3, i - 1] if i > 0 else xb_recv[r, 0]
            yy = s[1, i]
            gy = (
                (xy - behind)
                + (after_y(yy, row_of(ya_recv, r, 0, i)) - yy)
                + (yz - before_z(yz))
            )
            behind = s[4, i - 1] if i > 0 else xb_recv[r, 1]
            zz = s[2, i]
            gz = (
                (xz - behind)
                + (yz - before_y(yz, row_of(yb_recv, r, 1, i)))
                + (after_z(zz) - zz)
            )
            v[0, i] = v_old[0, i] + scale * gx
            v[1, i] = v_old[1, i] + scale * gy
            v[2, i] = v_old[2, i] + scale * gz
        at = step * 4
        for k in range(4):
            copy_corner(step, k).wait_recv()
        c_xy = corner_recv[at, 0:1, :]
        c_yy, c_xx = corner_recv[at + 1, 0:1, :], corner_recv[at + 1, 4:5, :]
        c_yz = corner_recv[at + 2, 0:1, :]
        c_xz = corner_recv[at + 3, 0:1, :]
        e = nx - 1
        rows_of = lambda buf, c: buf[r, c * nx:(c + 1) * nx, :]
        if step == 0:
            v_behind_x = xb_recv[r, 2] + scale_behind * xb_recv[r, 3]
            v_ahead_y = xa_recv[r, 1].astype(F32) + scale_ahead * xa_recv[r, 3].astype(F32)
            v_ahead_z = xa_recv[r, 2].astype(F32) + scale_ahead * xa_recv[r, 4].astype(F32)
            v_after_x = rows_of(ya_recv, 1) + scale_after * rows_of(ya_recv, 3)
            v_after_z = rows_of(ya_recv, 2) + scale_after * rows_of(ya_recv, 4)
            v_before_y = rows_of(yb_recv, 2) + scale_before * rows_of(yb_recv, 3)
        else:
            v_behind_x = xb_recv[r, 2]
            v_ahead_y, v_ahead_z = xa_recv[r, 1].astype(F32), xa_recv[r, 2].astype(F32)
            v_after_x, v_after_z = rows_of(ya_recv, 1), rows_of(ya_recv, 2)
            v_before_y = rows_of(yb_recv, 2)
        v_behind_x = v_behind_x + scale_behind * (s[0, 0] - only_y(c_xy, 0))
        v_ahead_y = v_ahead_y + scale_ahead * (only_y(c_yy, ny - 1) - s[3, e])
        v_ahead_z = v_ahead_z - scale_ahead * (only_y(c_yz, 0) + s[4, e])
        v_after_x = v_after_x + scale_after * (
            only_x(c_xx, e, next_y + PY < n) - s[3, :, ny - 1, :]
        )
        v_after_z = v_after_z - scale_after * (
            only_x(c_xz, 0, next_y >= PY) + s[5, :, ny - 1, :]
        )
        v_before_y = v_before_y + scale_before * (
            s[1, :, 0, :] - only_x(c_xy, 0, prev_y >= PY)
        )

        for i in order:
            lame, shear = LAM[i], MU[i]
            vx, vy, vz = v[0, i], v[1, i], v[2, i]
            behind = v[0, i - 1] if i > 0 else v_behind_x
            ex = vx - behind
            ey = vy - before_y(vy, v_before_y[i:i + 1])
            ez = vz - before_z(vz)
            spread = lame * (ex + ey + ez)
            ahead_y = v[1, i + 1] if i < nx - 1 else v_ahead_y
            ahead_z = v[2, i + 1] if i < nx - 1 else v_ahead_z
            rates = (
                spread + 2.0 * shear * ex,
                spread + 2.0 * shear * ey,
                spread + 2.0 * shear * ez,
                shear * ((after_y(vx, v_after_x[i:i + 1]) - vx) + (ahead_y - vy)),
                shear * ((after_z(vx) - vx) + (ahead_z - vz)),
                shear * ((after_z(vy) - vy) + (after_y(vz, v_after_z[i:i + 1]) - vz)),
            )
            keep = DEC[i]
            drop = (1.0 - keep) * LOS[i]
            for c in range(6):
                m = keep * M[c, i] - drop * rates[c]
                m_new[c, i] = m
                new = s[c, i] + COURANT * (rates[c] + m)
                s_new[c, i] = new + source[step, i] if c < 3 else new
            if not last and i == 0:
                send_first_partial(step + 1, s_new, v)
            if not last and i == nx - 1:
                send_last_partial(step + 1, s_new, v)
        if not last:
            send_y_partial(step + 1, s_new, v)
            send_corners(step + 1, s_new)

    pltpu.make_async_copy(packed.at[part], packed.at[part], tile_send).wait()
    pl.when(has_behind)(lambda: copy_table_a().wait_send())
    pl.when(has_ahead)(lambda: copy_table_b().wait_send())
    for r in range(steps):
        copy_ya(r).wait_send()
        copy_yb(r).wait_send()
        pl.when(has_behind)(functools.partial(lambda q: copy_xa(q).wait_send(), r))
        pl.when(has_ahead)(functools.partial(lambda q: copy_xb(q).wait_send(), r))
    for step in range(steps):
        for k in range(4):
            copy_corner(step, k).wait_send()


def write(v, s, m, out_v, out_s, out_m, sems):
    stores = [
        pltpu.make_async_copy(src, dst.at[:, 0], sems.at[k])
        for k, (src, dst) in enumerate(((s, out_s), (m, out_m), (v, out_v)))
    ]
    for store in stores:
        store.start()
    for store in stores:
        store.wait()


def body(n, velocity, stress, memory, lame_lambda, lame_mu, buoyancy, decay, loss,
         tile_lambda, tile_mu, tile_buoy, tile_dest, brick_tiles, src_index, src_wave):
    steps = src_wave.shape[1]
    grid = lame_lambda.shape[1:]
    nx, ny, nz = grid
    rounds = steps
    corners = 4 * steps
    hbm = pl.BlockSpec(memory_space=pltpu.HBM)
    vmem = pl.BlockSpec(memory_space=pltpu.VMEM)
    big = (velocity, stress, memory, lame_lambda, lame_mu, buoyancy, decay, loss)
    small = (tile_lambda, tile_mu, tile_buoy, tile_dest.reshape(1, -1), brick_tiles,
             src_index.reshape(1, -1), src_wave.T)
    states = pl.pallas_call(
        functools.partial(kernel, n, steps),
        out_shape=tuple(jax.ShapeDtypeStruct((c,) + grid, F32) for c in (3, 6, 6)),
        in_specs=[hbm] * (len(big) + len(small)),
        out_specs=(vmem,) * 3,
        scratch_shapes=[
            pltpu.VMEM((steps, 3) + grid, F32),
            pltpu.VMEM((steps, 6) + grid, F32),
            pltpu.VMEM((6,) + grid, F32),
        ] + [pltpu.VMEM(grid, F32)] * 5 + [pltpu.VMEM(a.shape, a.dtype) for a in small] + [
            pltpu.VMEM((n * TZ, 128), F32),
            pltpu.VMEM((n * TZ, 128), F32),
            pltpu.VMEM((steps,) + grid, F32),
            pltpu.VMEM((rounds, 6, ny, nz), jnp.bfloat16),
            pltpu.VMEM((rounds, 6, ny, nz), jnp.bfloat16),
            pltpu.VMEM((rounds, 6, ny, nz), F32),
            pltpu.VMEM((rounds, 6, ny, nz), F32),
        ] + [pltpu.VMEM((rounds, 32, nz), F32)] * 4
        + [pltpu.VMEM((corners, 8, nz), F32)] * 2 + [
            pltpu.VMEM((8, nz), F32),
            pltpu.VMEM((2, 8, nz), F32),
            pltpu.SemaphoreType.DMA((8,)),
            pltpu.SemaphoreType.DMA((len(small),)),
            pltpu.SemaphoreType.DMA,
            pltpu.SemaphoreType.DMA,
            pltpu.SemaphoreType.DMA((4 * rounds + 2,)),
            pltpu.SemaphoreType.DMA((4 * rounds + 2,)),
            pltpu.SemaphoreType.DMA((corners,)),
            pltpu.SemaphoreType.DMA((corners,)),
        ],
        compiler_params=pltpu.CompilerParams(
            collective_id=0, has_side_effects=True, vmem_limit_bytes=VMEM_LIMIT
        ),
    )(*big, *small)
    return pl.pallas_call(
        write,
        out_shape=tuple(
            jax.ShapeDtypeStruct(a.shape, F32) for a in (velocity, stress, memory)
        ),
        in_specs=[vmem] * 3,
        out_specs=(hbm,) * 3,
        scratch_shapes=[pltpu.SemaphoreType.DMA((3,))],
    )(*states)


def solution(mesh):
    both = ("groups", "gx")
    field = P(None, both, None, None, None)
    single = P(both, None, None, None)
    return jax.shard_map(
        functools.partial(body, mesh.shape["gx"]),
        mesh=mesh,
        in_specs=(field,) * 3 + (single,) * 5 + (P(both, None),) * 3
        + (P(both), P(both, None), P(both), P(both, None)),
        out_specs=(field,) * 3,
        check_vma=False,
    )
```
